32 devices in a mesh: tok: 8 (over y, x, core), head: 4 (over z).
Axes of the slice: x: 2, y: 2, z: 4, core: 2. Of those that a mesh axis runs over, the one named last changes fastest.
Arguments:
- tokens: bfloat16 [4096, 1536], P(('tok', 'head')), may hold values from -6 to 6
- segments: int32 [4096], replicated, may hold values from 0 to 63, never falling along the last dimension, each value on 1 to 512 neighbouring positions
- group_ids: int32 [64], replicated, may hold values from 0 to 7
- prefix_owner: int32 [8], replicated, may hold values from 0 to 7, each once
- slab_fill: int32 [8], replicated, may hold values from 256 to 512
- prefix_cache: bfloat16 [4096, 1024], P('tok', 'head'), may hold values from -400 to 400, as said below
- attn_gain: float32 [1536], replicated, may hold values from 0.5 to 1.5
- w_query: bfloat16 [1536, 1536], P(None, 'head'), may hold values from -0.15625 to 0.15625
- w_keyval: bfloat16 [1536, 1024], P(None, 'head'), may hold values from -0.15625 to 0.15625
- w_out: bfloat16 [1536, 1536], P('head'), may hold values from -0.15625 to 0.15625
- ffn_gain: float32 [1536], replicated, may hold values from 0.5 to 1.5
- routes: int32 [4096, 8], P(('tok', 'head')), may hold values from 0 to 31, all different within a row; in each aligned block of 128 rows (0 to 127, 128 to 255, ...) at most 64 rows name the same one
- route_gates: float32 [4096, 8], P(('tok', 'head')), may hold values from 0.05 to 0.5
- w_gate: bfloat16 [32, 1536, 512], P('tok'), may hold values from -0.15625 to 0.15625
- w_up: bfloat16 [32, 1536, 512], P('tok'), may hold values from -0.15625 to 0.15625
- w_down: bfloat16 [32, 512, 1536], P('tok'), may hold values from -0.25 to 0.25
Outputs:
- layer_out: bfloat16 [4096, 1536], P(('tok', 'head'))
The draws below stay inside these ranges and needn't reach their ends.
Inputs may be any that keep to these rules, and one draw needn't show every extreme that they name: `segments`: request ids never fall along the tokens; every request has 1 to 512 tokens and some request exactly 512. `prefix_owner`: each group's prefix lies in exactly one slab. `prefix_cache`: keys are already rotated by their positions 0 to fill - 1; rows at fill and past it are padding. `routes`: each row names 8 different experts; the rows of one device name any expert at most 64 times.
All inputs are finite; a program needn't handle non-finite values.
Results may differ from the reference program's by a relative error of at most 0.012.
Values may be sent and summed in bfloat16 or wider, within the bound.
No kernel may reach another device: no remote copies, remote signals or barrier semaphores. Data moves between devices by JAX's collectives and lax.ppermute only.
A program may use at most 192 MiB of HBM per device.

```python
import math
import jax
import jax.numpy as jnp
import numpy as np
from jax import lax

D = 1536
HQ = 24
KVH = 8
HS = 64
FF = 512
EXPERTS = 32
TOPK = 8
PREFIX = 512
TOK_DEV = 128
TOK_ROW = 512
TOKENS = 4096
REQS = 64
GROUPS = 8
CAP = 64


def draw_prefix_cache(key, part):
    base = jax.random.truncated_normal(key, -4.0, 4.0, (GROUPS, PREFIX, KVH, 2, HS), jnp.float32)
    level_key = jax.random.fold_in(key, 11)
    level = jax.random.uniform(level_key, (GROUPS, 1, 1, 1, 1), jnp.float32, math.log(0.5), math.log(2.0))
    factor = jnp.concatenate([jnp.exp(level), jnp.ones((GROUPS, 1, 1, 1, 1), jnp.float32)], axis=3)
    return (base * factor).reshape(GROUPS * PREFIX, KVH * 2 * HS).astype(jnp.bfloat16)


def plant(array, own_key, low, largest):
    spot = [jax.random.randint(jax.random.fold_in(own_key, axis), (), 0, length) for axis, length in enumerate(array.shape)]
    longest = array.shape.index(max(array.shape))
    neighbour = spot[:longest] + [(spot[longest] + 1) % array.shape[longest]] + spot[longest + 1:]
    return array.at[tuple(spot)].set(low).at[tuple(neighbour)].set(largest)


def block_levels(rng, extent, pieces, smallest, top_value):
    level, own = 1.0, jax.random.fold_in(rng, 6)
    for dim, blocks in pieces:
        heights = jnp.exp(jax.random.uniform(jax.random.fold_in(own, dim), (blocks,), jnp.float32, smallest / len(pieces), top_value / len(pieces)))
        level = level * jnp.repeat(heights, extent[dim] // blocks).reshape([-1 if axis == dim else 1 for axis in range(len(extent))])
    return level


def cumulative_ranks(count, slope):
    weights = [(1 << 20) // math.isqrt(grade ** slope) + 1 for grade in range(1, count + 1)]
    scale = 1 + sum(weights) // (1 << 30)
    return np.cumsum(np.array([max(1, weight // scale) for weight in weights]))


def ranked_ids(key, extent, count, slope):
    listing = cumulative_ranks(count, slope)
    lot = jax.random.randint(jax.random.fold_in(key, 1), extent, 0, int(listing[count - 1]))
    grade = jnp.searchsorted(jnp.asarray(listing, jnp.int32), lot, side="right")
    return jax.random.permutation(jax.random.fold_in(key, 2), count)[grade].astype(jnp.int32)


def split_up(number_of, total, most, lean):
    weights = [(1 << 20) // math.isqrt(standing ** lean) + 1 for standing in range(2, number_of + 1)]
    surplus, counts = total - most - (number_of - 1), [1] * (number_of - 1)
    while surplus > 0:
        candidates = [i for i in range(number_of - 1) if counts[i] < most]
        pool, remaining = sum([weights[i] for i in candidates]), surplus
        for i in candidates:
            extra = min(most - counts[i], max(1, remaining * weights[i] // pool), surplus)
            counts[i] = counts[i] + extra
            surplus = surplus - extra
    return np.array([most] + counts)


def ragged(rng, number_of, total, bound, lean):
    if number_of == 2:
        one = jax.random.randint(rng, (), max(1, total - bound), min(bound, total - 1) + 1)
        return jnp.stack([one, total - one])
    sizes = jnp.asarray(split_up(number_of, total, bound, lean), jnp.int32)
    couples = (number_of - 1) // 2
    giver, sink = sizes[1:1 + 2 * couples:2], sizes[2:2 + 2 * couples:2]
    room = jnp.minimum(giver - 1, bound - sink)
    passed = jax.random.randint(jax.random.fold_in(rng, 1), (couples,), 0, 1 << 20) % (room + 1)
    sizes = sizes.at[1:1 + 2 * couples:2].set(giver - passed).at[2:2 + 2 * couples:2].set(sink + passed)
    return sizes[jax.random.permutation(jax.random.fold_in(rng, 2), number_of)]


def shared_out(own_key, own, number, rows, number_of, top, limit, lean):
    sequence = jax.random.permutation(own_key, number_of)
    crowded, common = shares(number_of, rows * top, limit, lean, True), shares(number_of, rows * top, limit, lean, False)
    places = jnp.arange(number_of)

    def named(lengths, rotation):
        used = int((lengths > 0).sum())
        fixed = max(1, used // 4)
        shifted = fixed + (places - fixed + rotation * (used - fixed)) % max(1, number_of - fixed)
        return jnp.zeros((number_of,), jnp.int32).at[sequence[jnp.where(places < fixed, places, shifted)]].set(jnp.asarray(lengths, jnp.int32))

    lengths = jnp.where(number % 4 == 0, named(crowded, number // 4), named(common, number - number // 4 - 1))
    mixed = jax.random.permutation(jax.random.fold_in(own, 3), number_of)
    source_of, sink = mixed[0:number_of // 2 * 2:2], mixed[1:number_of // 2 * 2:2]
    margin = jnp.minimum(lengths[source_of] - 1, limit - lengths[sink]) // 2
    margin = jnp.where((source_of == sequence[0]) | (sink == sequence[0]) | (lengths[sink] == 0), 0, jnp.maximum(margin, 0))
    shifted = jax.random.randint(jax.random.fold_in(own, 4), (number_of // 2,), 0, 1 << 20) % (margin + 1)
    lengths = lengths.at[source_of].add(-shifted).at[sink].add(shifted)
    labels = jnp.searchsorted(jnp.cumsum(lengths), jnp.arange(rows * top), side="right").astype(jnp.int32)
    table = labels.reshape(top, rows).T
    table = table[jax.random.permutation(jax.random.fold_in(own, 1), rows)]
    rotation = jax.random.randint(jax.random.fold_in(own, 2), (rows, 1), 0, top)
    return jnp.take_along_axis(table, (jnp.arange(top)[None, :] + rotation) % top, axis=1)


def shares(amount, total, reach, lean, full):
    portions = [(1 << 20) // math.isqrt(rank ** lean) + 1 for rank in range(1, amount + 1)]
    largest = reach if full else min(reach, max(-(-total // amount), total * portions[0] // sum(portions)))
    least = 1 if total - largest >= amount - 1 else 0
    given, surplus = [largest] + [least] * (amount - 1), total - largest - least * (amount - 1)
    while surplus > 0:
        free = [i for i in range(1, amount) if given[i] < largest] or [i for i in range(1, amount) if given[i] < reach]
        pool, remaining = sum([portions[i] for i in free]), surplus
        for i in free:
            more = min(reach - given[i], max(1, remaining * portions[i] // pool), surplus)
            given[i] = given[i] + more
            surplus = surplus - more
    return np.array(given)


def noise(stream_key, shape, scale, most, shards=(), held_as=jnp.bfloat16):
    drawn = jax.random.normal(stream_key, shape, jnp.float32) * scale
    if len(shards) > 0:
        drawn = block_levels(stream_key, shape, shards, -0.22, 0.18) * drawn
    return jnp.clip(drawn, min=-most, max=most).astype(held_as)


def setup_inputs(seed: int = 0) -> dict:
    streams_of = jax.random.split(jax.random.key(seed), 17)
    tokens = noise(streams_of[0], (TOKENS, D), 1.0, 6.0, ((0, 32),))
    segments = jnp.searchsorted(jnp.cumsum(ragged(streams_of[1], REQS, TOKENS, TOK_ROW, 2)), jnp.arange(TOKENS), side="right").astype(jnp.int32)
    group_ids = plant(ranked_ids(streams_of[2], (REQS,), GROUPS, 2), jax.random.fold_in(streams_of[2], 3), 0, GROUPS - 1).astype(jnp.int32)
    prefix_owner = jax.random.permutation(streams_of[3], GROUPS).astype(jnp.int32)
    slab_fill = plant(jax.random.randint(streams_of[4], (GROUPS,), PREFIX // 2, PREFIX + 1), jax.random.fold_in(streams_of[4], 1), PREFIX // 2, PREFIX).astype(jnp.int32)
    prefix_cache = draw_prefix_cache(jax.random.fold_in(streams_of[16], 71), 0)
    attn_gain = jnp.clip(1.0 + 0.1 * jax.random.normal(streams_of[6], (D,), jnp.float32), 0.5, 1.5)
    w_query = noise(streams_of[7], (D, HQ * HS), D ** -0.5, 0.15625, ((1, 4),))
    w_keyval = noise(streams_of[8], (D, KVH * 2 * HS), D ** -0.5, 0.15625, ((1, 4),))
    w_out = noise(streams_of[9], (HQ * HS, D), (HQ * HS) ** -0.5, 0.15625, ((0, 4),))
    ffn_gain = jnp.clip(1.0 + 0.1 * jax.random.normal(streams_of[10], (D,), jnp.float32), 0.5, 1.5)
    routes_keys = jax.random.split(jax.random.fold_in(streams_of[11], 1), TOKENS // TOK_DEV)
    routes_turns = jax.random.permutation(jax.random.fold_in(streams_of[11], 3), TOKENS // TOK_DEV)
    routes = jax.vmap(lambda own, number: shared_out(jax.random.fold_in(streams_of[11], 2), own, number, TOK_DEV, EXPERTS, TOPK, CAP, 2))(routes_keys, routes_turns).reshape((TOKENS, TOPK))
    route_gates = jnp.clip(jnp.exp(math.log(0.5) - 2.3025851 * jax.random.uniform(streams_of[12], (TOKENS, TOPK), jnp.float32) ** block_levels(streams_of[12], (TOKENS, TOPK), ((0, 32),), -0.2, 0.2)), 0.05, 0.5)
    w_gate = noise(streams_of[13], (EXPERTS, D, FF), D ** -0.5, 0.15625, ((0, 8),))
    w_up = noise(streams_of[14], (EXPERTS, D, FF), D ** -0.5, 0.15625, ((0, 8),))
    w_down = noise(streams_of[15], (EXPERTS, FF, D), FF ** -0.5, 0.25, ((0, 8),))
    return dict(tokens=tokens, segments=segments, group_ids=group_ids, prefix_owner=prefix_owner, slab_fill=slab_fill, prefix_cache=prefix_cache, attn_gain=attn_gain, w_query=w_query, w_keyval=w_keyval, w_out=w_out, ffn_gain=ffn_gain, routes=routes, route_gates=route_gates, w_gate=w_gate, w_up=w_up, w_down=w_down)


NEG_FILL = -1e+30
NORM_EPS = 1e-06

def rms_scale(values, gain):
    widened = values.astype(jnp.float32)
    spread = lax.optimization_barrier(jnp.mean(widened * widened, axis=-1, keepdims=True))
    return widened * lax.rsqrt(spread + NORM_EPS) * gain

def lookup(table, index):
    entries = jnp.arange(table.shape[0], dtype=jnp.int32)
    return lax.optimization_barrier(jnp.sum(jnp.where(index[..., None] == entries, table, 0), axis=-1)).astype(jnp.int32)

def token_tables(segments, group_ids, prefix_owner, slab_fill):
    length_all = segments.shape[0]
    places = jnp.arange(length_all, dtype=jnp.int32)
    opening = jnp.concatenate([jnp.ones((1,), dtype=bool), segments[1:] != segments[:-1]])
    begins = lax.cummax(jnp.where(opening, places, 0), axis=0)
    slab_ids = lookup(prefix_owner, lookup(group_ids, segments))
    token_fill = lookup(slab_fill, slab_ids)
    return (slab_ids, token_fill, token_fill + places - begins)

def rope_angles(positions, head_size):
    steps_idx = jnp.arange(head_size // 2, dtype=jnp.float32)
    inverse = jnp.exp(steps_idx * (-2.0 * jnp.log(10000.0) / head_size))
    return positions.astype(jnp.float32)[:, None] * inverse[None, :]

def rotate(values, angles):
    halfway = values.shape[-1] // 2
    leading = values[..., :halfway]
    trailing = values[..., halfway:]
    cosine = jnp.cos(angles)[:, None, :]
    sine_v = jnp.sin(angles)[:, None, :]
    return jnp.concatenate([leading * cosine - trailing * sine_v, trailing * cosine + leading * sine_v], axis=-1)

def reference(tokens, segments, group_ids, prefix_owner, slab_fill, prefix_cache, attn_gain, w_query, w_keyval, w_out, ffn_gain, routes, route_gates, w_gate, w_up, w_down):
    group_share = HQ // KVH
    score_scale = HS ** (-0.5)
    normed = rms_scale(tokens, attn_gain).astype(jnp.bfloat16)
    slab_ids, token_fill, positions = token_tables(segments, group_ids, prefix_owner, slab_fill)
    angles = rope_angles(positions, HS)
    queries = jnp.dot(normed, w_query, preferred_element_type=jnp.float32).reshape(TOKENS, HQ, HS)
    keyval = jnp.dot(normed, w_keyval, preferred_element_type=jnp.float32).reshape(TOKENS, KVH, 2, HS)
    queries = rotate(queries, angles).astype(jnp.bfloat16).reshape(TOKENS, KVH, group_share, HS)
    keys_now = rotate(keyval[:, :, 0], angles).astype(jnp.bfloat16)
    values_now = keyval[:, :, 1].astype(jnp.bfloat16)
    cache_all = prefix_cache.reshape(GROUPS, PREFIX, KVH, 2, HS)
    window = TOK_ROW
    block_rows = TOK_DEV // 2
    keys_pad = jnp.concatenate([jnp.zeros((window, KVH, HS), jnp.bfloat16), keys_now], axis=0)
    values_pad = jnp.concatenate([jnp.zeros((window, KVH, HS), jnp.bfloat16), values_now], axis=0)
    segs_pad = jnp.concatenate([jnp.full((window,), -1, jnp.int32), segments], axis=0)

    def attend(first_row):
        first_row = first_row.astype(jnp.int32)
        query_blk = lax.dynamic_slice_in_dim(queries, first_row, block_rows, 0).astype(jnp.float32)
        query_seg = lax.dynamic_slice_in_dim(segments, first_row, block_rows, 0)
        query_pos = first_row + jnp.arange(block_rows, dtype=jnp.int32)
        query_slab = lax.dynamic_slice_in_dim(slab_ids, first_row, block_rows, 0)
        query_fill = lax.dynamic_slice_in_dim(token_fill, first_row, block_rows, 0)
        near_keys = lax.dynamic_slice_in_dim(keys_pad, first_row, window + block_rows, 0).astype(jnp.float32)
        near_vals = lax.dynamic_slice_in_dim(values_pad, first_row, window + block_rows, 0).astype(jnp.float32)
        near_segs = lax.dynamic_slice_in_dim(segs_pad, first_row, window + block_rows, 0)
        near_pos = first_row - window + jnp.arange(window + block_rows, dtype=jnp.int32)
        prefix_rows = cache_all[query_slab]
        prefix_keys = prefix_rows[:, :, :, 0].astype(jnp.float32)
        prefix_vals = prefix_rows[:, :, :, 1].astype(jnp.float32)
        far_scores = jnp.einsum('qgrd,qkgd->qgrk', query_blk, prefix_keys) * score_scale
        near_scores = jnp.einsum('qgrd,kgd->qgrk', query_blk, near_keys) * score_scale
        far_mask = (jnp.arange(PREFIX, dtype=jnp.int32)[None, :] < query_fill[:, None])[:, None, None, :]
        near_mask = ((near_segs[None, :] == query_seg[:, None]) & (near_pos[None, :] <= query_pos[:, None]))[:, None, None, :]
        far_scores = jnp.where(far_mask, far_scores, NEG_FILL)
        near_scores = jnp.where(near_mask, near_scores, NEG_FILL)
        peak_score = jnp.maximum(lax.optimization_barrier(jnp.max(far_scores, axis=-1)), lax.optimization_barrier(jnp.max(near_scores, axis=-1)))
        far_weights = jnp.where(far_mask, jnp.exp(far_scores - peak_score[..., None]), 0.0)
        near_weights = jnp.where(near_mask, jnp.exp(near_scores - peak_score[..., None]), 0.0)
        weight_sum = lax.optimization_barrier(jnp.sum(far_weights, axis=-1)) + lax.optimization_barrier(jnp.sum(near_weights, axis=-1))
        far_round = lax.optimization_barrier(far_weights.astype(jnp.bfloat16)).astype(jnp.float32)
        near_round = lax.optimization_barrier(near_weights.astype(jnp.bfloat16)).astype(jnp.float32)
        mixed_blk = jnp.einsum('qgrk,qkgd->qgrd', far_round, prefix_vals) + jnp.einsum('qgrk,kgd->qgrd', near_round, near_vals)
        mixed_blk = mixed_blk / weight_sum[..., None]
        return mixed_blk.reshape(block_rows, HQ * HS).astype(jnp.bfloat16)
    starts_all = jnp.arange(TOKENS // block_rows, dtype=jnp.int32) * block_rows
    mixed = lax.map(attend, starts_all).reshape(TOKENS, HQ * HS)
    hidden = tokens.astype(jnp.float32) + jnp.dot(mixed, w_out, preferred_element_type=jnp.float32)
    expert_in = rms_scale(hidden, ffn_gain).astype(jnp.bfloat16)
    capacity_rows = TOKENS // TOK_DEV * CAP

    def run_expert(summed, expert):
        chosen = routes == expert
        is_used = jnp.any(chosen, axis=1)
        weight_of = lax.optimization_barrier(jnp.sum(jnp.where(chosen, route_gates, 0.0), axis=1))
        picked = jnp.nonzero(is_used, size=capacity_rows, fill_value=0)[0].astype(jnp.int32)
        is_valid = jnp.arange(capacity_rows, dtype=jnp.int32) < jnp.sum(is_used.astype(jnp.int32))
        rows_in = expert_in[picked]
        gate_val = jnp.dot(rows_in, w_gate[expert], preferred_element_type=jnp.float32)
        up_val = jnp.dot(rows_in, w_up[expert], preferred_element_type=jnp.float32)
        inner_act = (jax.nn.silu(gate_val) * up_val).astype(jnp.bfloat16)
        result = jnp.dot(inner_act, w_down[expert], preferred_element_type=jnp.float32).astype(jnp.bfloat16)
        weighted = jnp.where(is_valid[:, None], result.astype(jnp.float32) * weight_of[picked][:, None], 0.0)
        return (summed.at[picked].add(weighted), None)
    summed, _ = lax.scan(run_expert, jnp.zeros((TOKENS, D), jnp.float32), jnp.arange(EXPERTS, dtype=jnp.int32))
    return (hidden + summed).astype(jnp.bfloat16)
```

```python
import functools

import jax
import jax.numpy as jnp
from jax import lax
from jax.experimental import pallas as pl
from jax.experimental.pallas import tpu as pltpu
from jax.sharding import PartitionSpec as P

HS = 64
CAP = 64
PREFIX = 512
LANES = 128
NEG_FILL = -1e30
NORM_EPS = 1e-06
F32 = jnp.float32
BF16 = jnp.bfloat16
VMEM_BYTES = 56 * 1024 * 1024


def vmem(*shape):
    return pl.BlockSpec(memory_space=pltpu.VMEM)


ANY = pl.BlockSpec(memory_space=pl.ANY)
SMEM = pl.BlockSpec(memory_space=pltpu.SMEM)


def params(**more):
    return pltpu.CompilerParams(vmem_limit_bytes=VMEM_BYTES, **more)


def lookup(table, index):
    entries = jnp.arange(table.shape[0], dtype=jnp.int32)
    return jnp.sum(jnp.where(index[..., None] == entries, table, 0), axis=-1)


def ring(block, axis, step):
    count = lax.axis_size(axis)
    route = [(i, (i + step) % count) for i in range(count)]
    held = [block]
    for _ in range(count - 1):
        held.append(lax.ppermute(held[-1], axis, route))
    return held


def cube_routes():
    first = [(t, t ^ (2 if t & 1 else 4)) for t in range(8)]
    second = [(t, t ^ (4 if t & 1 else 2)) for t in range(8)]
    partner = [(t, t ^ 1) for t in range(8)]
    return first, second, partner


def plane_origins():
    count = lax.axis_size("tok")
    if count != 8:
        return jnp.arange(count, dtype=jnp.int32)
    me = lax.axis_index("tok")
    one = jnp.where(me % 2 == 0, 4, 2)
    two = 6 - one
    other = me ^ 1
    return jnp.stack(
        [me, me ^ one, me ^ two, me ^ 6, other, other ^ two, other ^ one, other ^ 6]
    ).astype(jnp.int32)


def plane_gather(block, split, joined, ties=(None, None, None)):
    count = lax.axis_size("tok")
    rows = block.shape[0]
    if count != 8:
        whole = lax.all_gather(block, "tok", axis=0, tiled=True)
        return [[(whole, i * rows, rows)] for i in range(count)]
    first, second, partner = cube_routes()

    def to_partner(array):
        return lax.ppermute(array, "tok", partner)

    block = after(block, ties[0])
    half = rows // 2
    one = lax.ppermute(block, "tok", first)
    two = lax.ppermute(block, "tok", second)
    one, two = after((one, two), ties[1])
    if split:
        three = [
            lax.ppermute(one[:half], "tok", second),
            lax.ppermute(two[half:], "tok", first),
        ]
    else:
        three = [lax.ppermute(block, "tok", [(t, t ^ 6) for t in range(8)])]
    if not joined:
        mine = [[block], [one], [two], three]
        every = mine + [[to_partner(piece) for piece in pieces] for pieces in mine]
        return [[(piece, 0, piece.shape[0]) for piece in pieces] for pieces in every]
    if split:
        head = jnp.concatenate([block, one, two], axis=0)
        tail = jnp.concatenate(three, axis=0)
        sides = [(head, tail), (to_partner(head), to_partner(tail))]
        return [
            [(side[0], i * rows, rows)] if i < 3 else [(side[1], 0, rows)]
            for side in sides
            for i in range(4)
        ]
    every = after(jnp.concatenate([block, one, two] + three, axis=0), ties[2])
    return [
        [(side, i * rows, rows)] for side in (every, to_partner(every)) for i in range(4)
    ]


def flatten(blocks):
    arrays, spec = [], []
    for pieces in blocks:
        here = []
        for array, first, rows in pieces:
            known = [i for i, other in enumerate(arrays) if other is array]
            if not known:
                known = [len(arrays)]
                arrays.append(array)
            here.append((known[0], first, rows))
        spec.append(here)
    return arrays, spec


def row_ranges(pieces, first, count):
    base = 0
    for array, start, rows in pieces:
        low, high = max(first, base), min(first + count, base + rows)
        if low < high:
            yield array, start + low - base, low - first, high - low
        base += rows


def after(value, tie):
    return value if tie is None else lax.optimization_barrier((value, tie))[0]


def plane_sum(near, far, last, rows):
    count = lax.axis_size("tok")
    if count != 8:
        every = jnp.concatenate([near, far, last], axis=0)
        return lax.psum_scatter(every, "tok", scatter_dimension=0, tiled=True).astype(F32)
    first, second, partner = cube_routes()
    half = rows // 2
    got_last = lax.ppermute(last, "tok", partner)
    got = lax.ppermute(far, "tok", partner)
    three = (near[3 * rows :].astype(F32) + got_last.astype(F32)).astype(BF16)
    across_upper = lax.ppermute(three[:half], "tok", second)
    across_lower = lax.ppermute(three[half:], "tok", first)
    near, got = after((near, got), (across_upper, across_lower))

    def pair(block):
        here = slice(block * rows, (block + 1) * rows)
        return near[here].astype(F32) + got[here].astype(F32)

    nothing = jnp.zeros(across_upper.shape, F32)
    add_upper = jnp.concatenate([across_upper.astype(F32), nothing], axis=0)
    add_lower = jnp.concatenate([nothing, across_lower.astype(F32)], axis=0)
    along = lax.ppermute((pair(1) + add_upper).astype(BF16), "tok", first)
    beside = lax.ppermute((pair(2) + add_lower).astype(BF16), "tok", second)
    return pair(0) + beside.astype(F32) + along.astype(F32)


def project_kernel(blocks, kv_local, q_local, *refs):
    pieces = refs[:blocks]
    gain, wq, wkv, cos, sin = refs[blocks : blocks + 5]
    q_outs = refs[blocks + 5 : 2 * blocks + 5]
    kv_out, normed = refs[2 * blocks + 5 :]
    half = pieces[0].shape[0]
    for i, piece in enumerate(pieces):
        wide = piece[...].astype(F32)
        spread = jnp.mean(wide * wide, axis=-1, keepdims=True)
        normed[i * half : (i + 1) * half, :] = (
            wide * lax.rsqrt(spread + NORM_EPS) * gain[...]
        ).astype(BF16)
    share = q_local // kv_local
    rows = normed.shape[0]
    rows_dev = rows // blocks
    lane = lax.broadcasted_iota(jnp.int32, (rows, LANES), 1)
    low_half = lane % HS < HS // 2
    low_head = lane < HS

    def turned(values, cosine, sine):
        swapped = jnp.where(
            low_half, pltpu.roll(values, LANES - HS // 2, 1), pltpu.roll(values, HS // 2, 1)
        )
        return values * cosine + swapped * sine

    cosine = cos[...]
    sine = sin[...]
    keyval = jnp.dot(normed[...], wkv[...], preferred_element_type=F32)
    cosine_kv = jnp.where(low_head, cosine, 1.0)
    sine_kv = jnp.where(low_head, sine, 0.0)
    for g in range(kv_local):
        here = slice(g * LANES, (g + 1) * LANES)
        kv_out[:, here] = turned(keyval[:, here], cosine_kv, sine_kv).astype(BF16)
    queries = jnp.dot(normed[...], wq[...], preferred_element_type=F32)
    for pair in range(queries.shape[1] // LANES):
        both = turned(queries[:, pair * LANES : (pair + 1) * LANES], cosine, sine) * HS ** (-0.5)
        for odd in range(2):
            head = 2 * pair + odd
            if head >= q_local:
                continue
            alone = pltpu.roll(both, HS, 1) if odd else both
            alone = jnp.where(low_head, alone, 0.0).astype(BF16)
            group, slot = head // share, head % share
            for j in range(blocks):
                q_outs[j][group, slot * rows_dev : (slot + 1) * rows_dev, :] = alone[
                    j * rows_dev : (j + 1) * rows_dev
                ]


def project(pieces, gain, w_query, w_keyval, cos, sin, kv_local, q_local):
    blocks = len(pieces)
    rows_dev, width = pieces[0].shape
    share = q_local // kv_local
    outs = pl.pallas_call(
        functools.partial(project_kernel, blocks, kv_local, q_local),
        out_shape=[jax.ShapeDtypeStruct((kv_local, share * rows_dev, LANES), BF16)] * blocks
        + [jax.ShapeDtypeStruct((blocks * rows_dev, kv_local * LANES), BF16)],
        in_specs=[vmem()] * (blocks + 5),
        out_specs=[vmem()] * (blocks + 1),
        scratch_shapes=[pltpu.VMEM((blocks * rows_dev, width), BF16)],
        compiler_params=params(),
        cost_estimate=pl.CostEstimate(
            flops=4 * 10**9, bytes_accessed=4 * 10**6, transcendentals=blocks * rows_dev
        ),
        name="norm_project_rotate",
    )(*pieces, gain, w_query, w_keyval, cos.reshape(-1, LANES), sin.reshape(-1, LANES))
    return list(outs[:-1]), outs[-1]


def attend_kernel(
    first, blocks, near_parts, slab_spec, q_local, near_list, reach, slab_list, slab_count, fill, slab_id, place, info, *refs
):
    parts = near_list.shape[0]
    total_in = blocks + near_parts + 1 + max(array for [(array, _, _)] in slab_spec)
    q_refs = refs[:blocks]
    near_refs = refs[blocks : blocks + near_parts]
    slab_refs = refs[blocks + near_parts : total_in]
    outs = refs[total_in : total_in + blocks]
    q_all, near, far, scores, peak, total, accum, begin, owner, heads, sems, slab_sems = refs[
        total_in + blocks :
    ]
    kv_local, stack, _ = q_refs[0].shape
    rows_dev = info.shape[1]
    share = stack // rows_dev
    cuts = PREFIX // LANES
    window = parts + 1
    wide = (stack, LANES)
    lane = lax.broadcasted_iota(jnp.int32, (1, LANES), 1)

    def lanes(ref, g, rows, start=0):
        return ref.at[pl.ds(start, rows), pl.ds(g * LANES, LANES)]

    copies = [
        pltpu.make_async_copy(ref, q_all.at[i], sems.at[i, 0]) for i, ref in enumerate(q_refs)
    ]
    base = 0
    for i, ref in enumerate(near_refs):
        for g in range(kv_local):
            copies.append(
                pltpu.make_async_copy(
                    lanes(ref, g, ref.shape[0]),
                    near.at[g, pl.ds(base, ref.shape[0])],
                    sems.at[blocks + i, g],
                )
            )
        base += ref.shape[0]
    slab_copies = [
        pltpu.make_async_copy(
            lanes(slab_refs[array], g, rows, start),
            far.at[g, pl.ds(i * PREFIX, PREFIX)],
            slab_sems.at[i, g],
        )
        for i, [(array, start, rows)] in enumerate(slab_spec)
        for g in range(kv_local)
    ]
    for copy in copies + slab_copies:
        copy.start()
    for copy in copies + slab_copies:
        copy.wait()

    @pl.loop(0, blocks)
    def _(i):
        block = lax.rem(first + i, parts)
        columns = info[block]
        for ref, column in ((owner, 0), (begin, 1)):
            tall = jnp.concatenate([columns[:, column : column + 1]] * share, axis=0)
            ref[...] = jnp.broadcast_to(tall, wide)
        row = lax.broadcasted_iota(jnp.int32, wide, 0)
        order = row - lax.div(row, rows_dev) * rows_dev

        def rows_near(g, back):
            unit = near_list[block, back]
            return near[g, pl.ds(pl.multiple_of(unit * rows_dev, rows_dev), rows_dev), :]

        def rows_window(g, backs):
            return jnp.concatenate([rows_near(g, back) for back in backs], axis=0)

        def rows_far(g, slab):
            return far[g, pl.ds(pl.multiple_of(slab * PREFIX, PREFIX), PREFIX), :]

        def score(g, rows):
            return lax.dot_general(
                q_all[i, g], rows, (((1,), (1,)), ((), ())), preferred_element_type=F32
            )

        def near_scores(backs, opening):
            for g in range(kv_local):
                every = score(g, rows_window(g, backs))
                top = None if opening else peak[g]
                for at, back in enumerate(backs):
                    there = place[near_list[block, back]] + lane
                    seen = there >= begin[...]
                    if back == 0:
                        seen = seen & (lane <= order)
                    here = every[:, at * LANES : (at + 1) * LANES]
                    here = jnp.where(seen, here, NEG_FILL)
                    scores[g, back] = here
                    top = here if top is None else jnp.maximum(top, here)
                peak[g] = top

        def far_scores(slab):
            mine = owner[...] == slab_id[slab]
            for g in range(kv_local):
                every = score(g, rows_far(g, slab))
                top = None
                for c in range(cuts):
                    here = every[:, c * LANES : (c + 1) * LANES]
                    if (c + 1) * LANES > PREFIX // 2:
                        here = jnp.where(lane + c * LANES < fill[slab], here, NEG_FILL)
                    scores[g, window + slab * cuts + c] = here
                    top = here if top is None else jnp.maximum(top, here)
                old = peak[g]
                peak[g] = jnp.where(mine, jnp.maximum(old, top), old)

        def near_values(backs, opening):
            for g in range(kv_local):
                weights = [jnp.exp(scores[g, back] - peak[g]) for back in backs]
                packed = jnp.concatenate([part.astype(BF16) for part in weights], axis=1)
                summed = functools.reduce(jnp.add, weights)
                mixed = jnp.dot(packed, rows_window(g, backs), preferred_element_type=F32)
                if opening:
                    total[g] = summed
                    accum[g] = mixed
                else:
                    total[g] += summed
                    accum[g] += mixed

        def far_values(slab):
            mine = owner[...] == slab_id[slab]
            for g in range(kv_local):
                shift = jnp.where(mine, peak[g], -NEG_FILL)
                weights = [
                    jnp.exp(scores[g, window + slab * cuts + c] - shift) for c in range(cuts)
                ]
                packed = jnp.concatenate([part.astype(BF16) for part in weights], axis=1)
                total[g] += functools.reduce(jnp.add, weights)
                accum[g] += jnp.dot(packed, rows_far(g, slab), preferred_element_type=F32)

        def sweep(near_body, far_body):
            near_body((0, 1), True)

            @pl.when(reach[block] != 0)
            def _():
                near_body(tuple(range(2, window)), False)

            @pl.loop(0, slab_count[block])
            def _(turn):
                far_body(slab_list[block, turn])

        sweep(near_scores, far_scores)
        for g in range(kv_local):
            peak[g] = jnp.broadcast_to(jnp.max(peak[g], axis=1, keepdims=True), wide)
        sweep(near_values, far_values)
        for g in range(kv_local):
            result = accum[g] / jnp.sum(total[g], axis=1, keepdims=True)
            for slot in range(share):
                heads[g * share + slot] = result[slot * rows_dev : (slot + 1) * rows_dev]

        low = lax.broadcasted_iota(jnp.int32, (rows_dev, LANES), 1) < HS
        done = []
        for pair in range((q_local + 1) // 2):
            left = pltpu.roll(heads[2 * pair], HS, 1)
            if 2 * pair + 1 < q_local:
                done.append(jnp.where(low, left, heads[2 * pair + 1]).astype(BF16))
            else:
                done.append(left[:, :HS].astype(BF16))
        for j in range(blocks):
            @pl.when(i == j)
            def _(j=j):
                for pair, part in enumerate(done):
                    outs[j][:, pair * LANES : pair * LANES + part.shape[1]] = part


def attend(first, tables, info, queries, near, slabs, q_local):
    blocks = len(queries)
    parts = info.shape[0]
    kv_local, stack, _ = queries[0].shape
    rows_dev = info.shape[1]
    units = parts + 1 + len(slabs) * (PREFIX // LANES)
    arrays, slab_spec = flatten(slabs)
    wide = (stack, LANES)
    return pl.pallas_call(
        functools.partial(attend_kernel, first, blocks, len(near), slab_spec, q_local),
        out_shape=[jax.ShapeDtypeStruct((rows_dev, q_local * HS), BF16)] * blocks,
        in_specs=[SMEM] * 7 + [vmem()] + [ANY] * (blocks + len(near) + len(arrays)),
        out_specs=[vmem()] * blocks,
        scratch_shapes=[
            pltpu.VMEM((blocks,) + queries[0].shape, BF16),
            pltpu.VMEM((kv_local, 2 * parts * rows_dev, LANES), BF16),
            pltpu.VMEM((kv_local, len(slabs) * PREFIX, LANES), BF16),
            pltpu.VMEM((kv_local, units) + wide, F32),
            pltpu.VMEM((kv_local,) + wide, F32),
            pltpu.VMEM((kv_local,) + wide, F32),
            pltpu.VMEM((kv_local,) + wide, F32),
            pltpu.VMEM(wide, jnp.int32),
            pltpu.VMEM(wide, jnp.int32),
            pltpu.VMEM((q_local, rows_dev, LANES), F32),
            pltpu.SemaphoreType.DMA((blocks + len(near), kv_local)),
            pltpu.SemaphoreType.DMA((len(slabs), kv_local)),
        ],
        compiler_params=params(),
        cost_estimate=pl.CostEstimate(
            flops=12 * 10**9, bytes_accessed=4 * 10**6, transcendentals=10**6
        ),
        name="attend",
    )(
        tables["near_list"],
        tables["reach"],
        tables["slab_list"],
        tables["slab_count"],
        tables["fill"],
        tables["slab_id"],
        tables["place"],
        info,
        *queries,
        *near,
        *arrays,
    )


def out_kernel(groups, cut, spec, origins, *refs):
    pieces = refs[:groups]
    w_own = refs[groups]
    w_far = refs[groups + 1 : -7]
    tokens, gain, hidden, expert_in, weights, sems, own_sem = refs[-7:]
    own = pltpu.make_async_copy(w_own, weights.at[0], own_sem)
    own.start()
    copies = []
    for k, pieces_k in enumerate(spec):
        if cut:
            first = pl.multiple_of(origins[k] * cut, 16)
            for j in range(groups - 1):
                for i, (array, there, offset, rows) in enumerate(
                    row_ranges(pieces_k, j * cut, cut)
                ):
                    copies.append(
                        pltpu.make_async_copy(
                            w_far[array].at[pl.ds(there, rows)],
                            weights.at[j + 1, pl.ds(first + offset, rows)],
                            sems.at[k, 2 * j + i],
                        )
                    )
        else:
            copies.append(
                pltpu.make_async_copy(w_far[pieces_k[0][0]], weights.at[k + 1], sems.at[k, 0])
            )
    for copy in copies:
        copy.start()
    own.wait()
    total = tokens[...].astype(F32) + jnp.dot(
        pieces[0][...], weights[0], preferred_element_type=F32
    )
    for copy in copies:
        copy.wait()
    for j in range(1, groups):
        total += jnp.dot(pieces[j][...], weights[j], preferred_element_type=F32)
    hidden[...] = total
    spread = jnp.mean(total * total, axis=-1, keepdims=True)
    expert_in[...] = (total * lax.rsqrt(spread + NORM_EPS) * gain[...]).astype(BF16)


def project_out(pieces, w_own, w_far, cut, origins, tokens, gain):
    groups = len(pieces)
    rows, width = tokens.shape
    w_far, spec = flatten(w_far)
    return pl.pallas_call(
        functools.partial(out_kernel, groups, cut, spec),
        out_shape=(
            jax.ShapeDtypeStruct((rows, width), F32),
            jax.ShapeDtypeStruct((rows, width), BF16),
        ),
        in_specs=[SMEM] + [vmem()] * groups + [ANY] * (1 + len(w_far)) + [vmem(), vmem()],
        out_specs=(vmem(), vmem()),
        scratch_shapes=[
            pltpu.VMEM((groups,) + w_own.shape, BF16),
            pltpu.SemaphoreType.DMA((len(spec), 2 * groups)),
            pltpu.SemaphoreType.DMA,
        ],
        compiler_params=params(),
        cost_estimate=pl.CostEstimate(
            flops=5 * 10**9,
            bytes_accessed=2 * groups * w_own.size + 8 * rows * width,
            transcendentals=rows,
        ),
        name="project_out_norm",
    )(origins, *pieces, w_own, *w_far, tokens, gain)


def expert_kernel(spec, rows, slot_row, gate_row, slot_col, *refs):
    count = len(spec)
    many = len(refs) - 15
    x_refs = refs[:many]
    wg_ref, wu_ref, wd_ref, near, far, last = refs[many : many + 6]
    x_all, wg, wu, wd, picked, answered, inner, x_sem, w_sem = refs[many + 6 :]
    exp_local = wg.shape[0]
    width = x_all.shape[1]
    span = 2 * rows
    slots = 2 * CAP
    pairs = count // 2
    chunk = 512

    x_copies = []
    base = 0
    for array, there, many_rows in [piece for pieces in spec for piece in pieces]:
        x_copies.append(
            pltpu.make_async_copy(
                x_refs[array].at[pl.ds(there, many_rows)],
                x_all.at[pl.ds(base, many_rows)],
                x_sem.at[len(x_copies)],
            )
        )
        base += many_rows
    for copy in x_copies:
        copy.start()

    def w_copies(e):
        return [
            pltpu.make_async_copy(source.at[e], target.at[e], w_sem.at[e, i])
            for i, (source, target) in enumerate(((wg_ref, wg), (wu_ref, wu), (wd_ref, wd)))
        ]

    for e in range(exp_local):
        for copy in w_copies(e):
            copy.start()
    for copy in x_copies:
        copy.wait()

    slot_iota = lax.broadcasted_iota(jnp.int32, (slots, span), 0)

    def pair_hits(e, b):
        there = slice(b * span, (b + 1) * span)
        return slot_iota == slot_row[pl.ds(e, 1), there]

    for b in range(pairs):
        hits = [jnp.where(pair_hits(e, b), 1.0, 0.0).astype(BF16) for e in range(exp_local)]
        chooser = jnp.concatenate(hits, axis=0)
        for c in range(0, width, chunk):
            found = jnp.dot(
                chooser,
                x_all[b * span : (b + 1) * span, c : c + chunk],
                preferred_element_type=F32,
            ).astype(BF16)
            for e in range(exp_local):
                picked[e, b * slots : (b + 1) * slots, c : c + chunk] = found[
                    e * slots : (e + 1) * slots
                ]

    @pl.loop(0, exp_local)
    def _(e):
        for copy in w_copies(e):
            copy.wait()
        rows_in = picked[e]
        for c in range(0, inner.shape[1], 256):
            gate = jnp.dot(rows_in, wg[e, :, c : c + 256], preferred_element_type=F32)
            up = jnp.dot(rows_in, wu[e, :, c : c + 256], preferred_element_type=F32)
            inner[:, c : c + 256] = (gate / (1.0 + jnp.exp(-gate)) * up).astype(BF16)
        scale = jnp.concatenate(
            [
                jnp.sum(
                    jnp.where(
                        pair_hits(e, b), gate_row[pl.ds(e, 1), b * span : (b + 1) * span], 0.0
                    ),
                    axis=1,
                    keepdims=True,
                )
                for b in range(pairs)
            ],
            axis=0,
        )
        for c in range(0, width, chunk):
            answer = jnp.dot(inner[...], wd[e, :, c : c + chunk], preferred_element_type=F32)
            answer = (answer * scale).astype(BF16)
            for b in range(pairs):
                first = pl.multiple_of(e * slots, slots)
                answered[b, pl.ds(first, slots), c : c + chunk] = answer[
                    b * slots : (b + 1) * slots
                ]

    lane = lax.broadcasted_iota(jnp.int32, (span, slots), 1)
    for b in range(pairs):
        there = slice(b * span, (b + 1) * span)
        spreader = jnp.concatenate(
            [
                jnp.where(lane == slot_col[there, e : e + 1], 1.0, 0.0).astype(BF16)
                for e in range(exp_local)
            ],
            axis=1,
        )
        for c in range(0, width, chunk):
            sums = jnp.dot(
                spreader, answered[b, :, c : c + chunk], preferred_element_type=F32
            ).astype(BF16)
            base = (b - pairs // 2) * span
            if b < pairs // 2:
                near[b * span : (b + 1) * span, c : c + chunk] = sums
            elif b < pairs - 1:
                far[base : base + span, c : c + chunk] = sums
            else:
                far[base : base + rows, c : c + chunk] = sums[:rows]
                last[:, c : c + chunk] = sums[rows:]


def experts(blocks, slot_row, gate_row, slot_col, w_gate, w_up, w_down):
    count = len(blocks)
    pieces, spec = flatten(blocks)
    parts = sum(len(one) for one in spec)
    rows, width = blocks[0][0][2], pieces[0].shape[1]
    exp_local, _, hidden = w_gate.shape
    pairs = count // 2
    slots = 2 * CAP
    work = exp_local * pairs * slots
    return pl.pallas_call(
        functools.partial(expert_kernel, spec, rows),
        out_shape=tuple(
            jax.ShapeDtypeStruct((many * rows, width), BF16)
            for many in (count // 2, count // 2 - 1, 1)
        ),
        in_specs=[vmem()] * 3 + [ANY] * (len(pieces) + 3),
        out_specs=(vmem(), vmem(), vmem()),
        scratch_shapes=[
            pltpu.VMEM((count * rows, width), BF16),
            pltpu.VMEM(w_gate.shape, BF16),
            pltpu.VMEM(w_up.shape, BF16),
            pltpu.VMEM(w_down.shape, BF16),
            pltpu.VMEM((exp_local, pairs * slots, width), BF16),
            pltpu.VMEM((pairs, exp_local * slots, width), BF16),
            pltpu.VMEM((pairs * slots, hidden), BF16),
            pltpu.SemaphoreType.DMA((parts,)),
            pltpu.SemaphoreType.DMA((exp_local, 3)),
        ],
        compiler_params=params(),
        cost_estimate=pl.CostEstimate(
            flops=2 * work * width * (3 * hidden + 4 * rows),
            bytes_accessed=2 * (3 * w_gate.size + 2 * count * rows * width),
            transcendentals=work * hidden,
        ),
        name="experts",
    )(slot_row, gate_row, slot_col, *pieces, w_gate, w_up, w_down)


def packed_routes(routes, route_gates, lanes):
    parts = [routes.T.astype(BF16)]
    rest = route_gates.T
    for _ in range(3):
        term = lax.reduce_precision(rest, 8, 7)
        parts.append(term.astype(BF16))
        rest = rest - term
    per = len(parts) * LANES // lanes
    return jnp.concatenate(
        [jnp.concatenate(parts[i : i + per], axis=0) for i in range(0, len(parts), per)], axis=1
    )


def route_kernel(spec, first_expert, *refs):
    count = len(spec)
    sources = refs[:-5]
    slot_row, gate_row, slot_col, packed, sems = refs[-5:]
    exp_local = slot_row.shape[0]
    tall = packed.shape[1]
    copies = [
        pltpu.make_async_copy(
            sources[array].at[pl.ds(there + rows - tall, tall), pl.ds(0, packed.shape[2])],
            packed.at[k],
            sems.at[k],
        )
        for k, (array, there, rows) in enumerate(pieces[-1] for pieces in spec)
    ]
    for copy in copies:
        copy.start()
    for copy in copies:
        copy.wait()
    here = lax.broadcasted_iota(jnp.int32, (LANES, LANES), 1)
    there = lax.broadcasted_iota(jnp.int32, (LANES, LANES), 0)
    earlier = jnp.where(there < here, 1.0, 0.0).astype(BF16)
    choices = tall * packed.shape[2] // (4 * LANES)
    for k in range(count):
        block = packed[k].astype(F32)
        parts = [
            block[r : r + choices, c : c + LANES]
            for c in range(0, packed.shape[2], LANES)
            for r in range(0, tall, choices)
        ]
        named = parts[0]
        gates = parts[1] + parts[2] + parts[3]
        hits, shares = [], []
        for e in range(exp_local):
            match = named == (first_expert[0] + e).astype(F32)
            hits.append(jnp.max(jnp.where(match, 1.0, 0.0), axis=0, keepdims=True))
            shares.append(jnp.sum(jnp.where(match, gates, 0.0), axis=0, keepdims=True))
        hits += [jnp.zeros((1, LANES), F32)] * (8 - exp_local)
        hit = jnp.concatenate(hits, axis=0)
        rank = jnp.dot(hit.astype(BF16), earlier, preferred_element_type=F32)
        slot = jnp.where(hit > 0.0, rank + float(k % 2 * CAP), -1.0)
        lanes = slice(k * LANES, (k + 1) * LANES)
        slot_row[:, lanes] = slot[:exp_local].astype(jnp.int32)
        gate_row[:, lanes] = jnp.concatenate(shares, axis=0)
        slot_col[lanes, :] = slot.T.astype(jnp.int32)


def route_tables(sources, tall, lanes, first_expert, exp_local):
    count = len(sources)
    sources, spec = flatten(sources)
    tokens = count * LANES
    return pl.pallas_call(
        functools.partial(route_kernel, spec),
        out_shape=(
            jax.ShapeDtypeStruct((exp_local, tokens), jnp.int32),
            jax.ShapeDtypeStruct((exp_local, tokens), F32),
            jax.ShapeDtypeStruct((tokens, 8), jnp.int32),
        ),
        in_specs=[SMEM] + [ANY] * len(sources),
        out_specs=(vmem(), vmem(), vmem()),
        scratch_shapes=[
            pltpu.VMEM((count, tall, lanes), BF16),
            pltpu.SemaphoreType.DMA((count,)),
        ],
        compiler_params=params(),
        cost_estimate=pl.CostEstimate(
            flops=3 * 10**9, bytes_accessed=10**6, transcendentals=0
        ),
        name="route_tables",
    )(first_expert, *sources)


def local(
    tokens,
    segments,
    group_ids,
    prefix_owner,
    slab_fill,
    prefix_cache,
    attn_gain,
    w_query,
    w_keyval,
    w_out,
    ffn_gain,
    routes,
    route_gates,
    w_gate,
    w_up,
    w_down,
):
    tok_count = lax.axis_size("tok")
    groups = lax.axis_size("head")
    me_tok = lax.axis_index("tok")
    me_head = lax.axis_index("head")
    rows_dev, width = tokens.shape
    row_len = rows_dev * groups
    row_first = me_tok * row_len
    kv_local = w_keyval.shape[1] // (2 * HS)
    q_local = w_query.shape[1] // HS
    origins = plane_origins()

    turns = ring(tokens, "head", 1)

    steps = jnp.arange(groups, dtype=jnp.int32)
    block_of = (me_head - steps) % groups
    token_id = row_first + block_of[:, None] * rows_dev + jnp.arange(rows_dev, dtype=jnp.int32)
    row_segs = lax.dynamic_slice_in_dim(segments, row_first, row_len, 0).reshape(groups, rows_dev)
    segs = jnp.sum(
        jnp.where((block_of[:, None] == steps[None, :])[:, :, None], row_segs[None], 0), axis=1
    )
    requests = jnp.arange(group_ids.shape[0], dtype=jnp.int32)
    starts = jnp.sum((segments[None, :] < requests[:, None]).astype(jnp.int32), axis=1)
    begin = lookup(starts, segs)
    slab = lookup(lookup(prefix_owner, group_ids), segs)
    fill = lookup(slab_fill, slab)
    position = fill + token_id - begin
    steps_idx = jnp.arange(HS // 2, dtype=F32)
    inverse = jnp.exp(steps_idx * (-2.0 * jnp.log(10000.0) / HS))
    angles = position.astype(F32)[:, :, None] * inverse
    cosine = jnp.cos(angles)
    sine = jnp.sin(angles)
    cos = jnp.concatenate([cosine] * 4, axis=2)
    sin = jnp.concatenate([-sine, sine, -sine, sine], axis=2)
    info = jnp.stack([slab, begin, token_id, token_id], axis=2)
    place = token_id[:, 0]
    backs = jnp.arange(groups + 1, dtype=jnp.int32)
    read = jnp.any(slab[:, :, None] == origins, axis=1).astype(jnp.int32)
    spot = jnp.arange(read.shape[1], dtype=jnp.int32)
    rank = jnp.sum(jnp.where(spot[:, None] < spot[None, :], read[:, :, None], 0), axis=1)
    tables = {
        "near_list": (steps[:, None] + backs[None, :]) % groups
        + jnp.where(block_of[:, None] >= backs[None, :], groups, 0),
        "reach": (begin[:, 0] < place - rows_dev).astype(jnp.int32),
        "slab_list": jnp.sum(
            jnp.where(
                (rank[:, :, None] == spot[None, None, :]) & (read[:, :, None] != 0),
                spot[None, :, None],
                0,
            ),
            axis=1,
        ),
        "slab_count": jnp.sum(read, axis=1),
        "fill": lookup(slab_fill, origins),
        "slab_id": origins,
        "place": jnp.concatenate([place - row_len, place]),
    }

    missing = -w_query.shape[1] % LANES
    if missing:
        w_query = jnp.pad(w_query, ((0, 0), (0, missing)))
    queries, own, prev = [], [], []
    for some in (slice(0, groups - 1), slice(groups - 1, groups)):
        query, keyval = project(
            after(turns[some], own[0]) if own else turns[some],
            attn_gain[None, :],
            w_query,
            w_keyval,
            cos[some],
            sin[some],
            kv_local,
            q_local,
        )
        queries += query
        own.append(keyval)
        prev.append(lax.ppermute(keyval, "tok", [(i, i + 1) for i in range(tok_count - 1)]))

    cached = plane_gather(prefix_cache, False, True, [turns[1], None, own[0]])

    def exchanged(block, j):
        return lax.ppermute(block, "head", [(i, (i - j) % groups) for i in range(groups)])

    near = prev + own
    cut = w_out.shape[0] // tok_count if tok_count == 8 else 0
    share = lax.dynamic_slice_in_dim(w_out, me_tok * cut, cut, 0) if cut else w_out
    share = after(share, own[-1])
    w_far = [exchanged(share, s) for s in range(1, groups)]
    middle = groups // 2
    early = attend(1, tables, info, queries[1 : middle + 1], near, cached, q_local)
    late = attend(
        middle + 1, tables, info, queries[middle + 1 :] + queries[:1], near, cached, q_local
    )
    mixed = [exchanged(block, 1 + i) for i, block in enumerate(early)]
    packed = packed_routes(routes, route_gates, 2 * LANES)
    if cut:
        w_far = after(w_far, early[0])
        packed = jnp.pad(packed, ((0, 0), (0, width - packed.shape[1])))
        w_far = plane_gather(
            jnp.concatenate(w_far + [packed], axis=0), True, True, [None, (late[0], mixed), None]
        )
        route_parts = w_far
    else:
        route_parts = plane_gather(packed, False, False)
        w_far = [[(block, 0, block.shape[0])] for block in w_far]
    exp_local = w_gate.shape[0]
    route = route_tables(
        route_parts,
        packed.shape[0],
        2 * LANES,
        (me_tok * exp_local).astype(jnp.int32).reshape(1),
        exp_local,
    )
    mixed += [exchanged(block, middle + 1 + i) for i, block in enumerate(late[:-1])]
    mixed = [late[-1]] + mixed
    hidden, expert_in = project_out(
        mixed, w_out, w_far, cut, origins, tokens, ffn_gain[None, :]
    )
    blocks = plane_gather(expert_in, True, False, [None, route[0], None])
    near, far, last = experts(blocks, *route, w_gate, w_up, w_down)
    return (hidden + plane_sum(near, far, last, rows_dev)).astype(BF16)


def solution(mesh):
    return jax.shard_map(
        local,
        mesh=mesh,
        in_specs=(
            P(("tok", "head"), None),
            P(),
            P(),
            P(),
            P(),
            P("tok", "head"),
            P(),
            P(None, "head"),
            P(None, "head"),
            P("head", None),
            P(),
            P(("tok", "head"), None),
            P(("tok", "head"), None),
            P("tok", None, None),
            P("tok", None, None),
            P("tok", None, None),
        ),
        out_specs=P(("tok", "head"), None),
        check_vma=False,
    )
```

```python
import functools

import jax
import jax.numpy as jnp
from jax import lax
from jax.experimental import pallas as pl
from jax.experimental.pallas import tpu as pltpu
from jax.sharding import PartitionSpec as P

HS = 64
CAP = 64
PREFIX = 512
LANES = 128
NEG_FILL = -1e30
NORM_EPS = 1e-06
F32 = jnp.float32
BF16 = jnp.bfloat16
VMEM_BYTES = 56 * 1024 * 1024


def vmem(*shape):
    return pl.BlockSpec(memory_space=pltpu.VMEM)


ANY = pl.BlockSpec(memory_space=pl.ANY)
SMEM = pl.BlockSpec(memory_space=pltpu.SMEM)


def params(**more):
    return pltpu.CompilerParams(vmem_limit_bytes=VMEM_BYTES, **more)


def lookup(table, index):
    entries = jnp.arange(table.shape[0], dtype=jnp.int32)
    return jnp.sum(jnp.where(index[..., None] == entries, table, 0), axis=-1)


def next_turn(block, axis):
    count = lax.axis_size(axis)
    return lax.ppermute(block, axis, [(i, (i + 1) % count) for i in range(count)])


def cube_routes():
    first = [(t, t ^ (2 if t & 1 else 4)) for t in range(8)]
    second = [(t, t ^ (4 if t & 1 else 2)) for t in range(8)]
    partner = [(t, t ^ 1) for t in range(8)]
    return first, second, partner


def plane_origins():
    count = lax.axis_size("tok")
    if count != 8:
        return jnp.arange(count, dtype=jnp.int32)
    me = lax.axis_index("tok")
    one = jnp.where(me % 2 == 0, 4, 2)
    two = 6 - one
    other = me ^ 1
    return jnp.stack(
        [me, me ^ one, me ^ two, me ^ 6, other, other ^ two, other ^ one, other ^ 6]
    ).astype(jnp.int32)


def plane_gather(block, split, joined, ties=(None, None, None)):
    count = lax.axis_size("tok")
    rows = block.shape[0]
    if count != 8:
        whole = lax.all_gather(block, "tok", axis=0, tiled=True)
        return [[(whole, i * rows, rows)] for i in range(count)]
    first, second, partner = cube_routes()

    def to_partner(array):
        return lax.ppermute(array, "tok", partner)

    block = after(block, ties[0])
    half = rows // 2
    one = lax.ppermute(block, "tok", first)
    two = lax.ppermute(block, "tok", second)
    one, two = after((one, two), ties[1])
    if split:
        three = [
            lax.ppermute(one[:half], "tok", second),
            lax.ppermute(two[half:], "tok", first),
        ]
    else:
        three = [lax.ppermute(block, "tok", [(t, t ^ 6) for t in range(8)])]
    if not joined:
        mine = [[block], [one], [two], three]
        every = mine + [[to_partner(piece) for piece in pieces] for pieces in mine]
        return [[(piece, 0, piece.shape[0]) for piece in pieces] for pieces in every]
    every = jnp.concatenate(after([block, one, two] + three, ties[2]), axis=0)
    return [
        [(side, i * rows, rows)] for side in (every, to_partner(every)) for i in range(4)
    ]


def flatten(blocks):
    arrays, spec = [], []
    for pieces in blocks:
        here = []
        for array, first, rows in pieces:
            known = [i for i, other in enumerate(arrays) if other is array]
            if not known:
                known = [len(arrays)]
                arrays.append(array)
            here.append((known[0], first, rows))
        spec.append(here)
    return arrays, spec


def row_ranges(pieces, first, count):
    base = 0
    for array, start, rows in pieces:
        low, high = max(first, base), min(first + count, base + rows)
        if low < high:
            yield array, start + low - base, low - first, high - low
        base += rows


def after(value, tie):
    return value if tie is None else lax.optimization_barrier((value, tie))[0]


def plane_sum(near, far, last, rows):
    count = lax.axis_size("tok")
    if count != 8:
        every = jnp.concatenate([near, far, last], axis=0)
        return lax.psum_scatter(every, "tok", scatter_dimension=0, tiled=True).astype(F32)
    first, second, partner = cube_routes()
    half = rows // 2
    got_last = lax.ppermute(last, "tok", partner)
    got = lax.ppermute(far, "tok", partner)
    three = (near[3 * rows :].astype(F32) + got_last.astype(F32)).astype(BF16)
    across_upper = lax.ppermute(three[:half], "tok", second)
    across_lower = lax.ppermute(three[half:], "tok", first)
    near, got = after((near, got), (across_upper, across_lower))

    def pair(block):
        here = slice(block * rows, (block + 1) * rows)
        return near[here].astype(F32) + got[here].astype(F32)

    nothing = jnp.zeros(across_upper.shape, F32)
    add_upper = jnp.concatenate([across_upper.astype(F32), nothing], axis=0)
    add_lower = jnp.concatenate([nothing, across_lower.astype(F32)], axis=0)
    along = lax.ppermute((pair(1) + add_upper).astype(BF16), "tok", first)
    beside = lax.ppermute((pair(2) + add_lower).astype(BF16), "tok", second)
    return pair(0) + beside.astype(F32) + along.astype(F32)


def project_kernel(blocks, kv_local, q_local, *refs):
    pieces = refs[:blocks]
    gain, wq, wkv, cos, sin = refs[blocks : blocks + 5]
    q_outs = refs[blocks + 5 : 2 * blocks + 5]
    kv_out, normed = refs[2 * blocks + 5 :]
    half = pieces[0].shape[0]
    for i, piece in enumerate(pieces):
        wide = piece[...].astype(F32)
        spread = jnp.mean(wide * wide, axis=-1, keepdims=True)
        normed[i * half : (i + 1) * half, :] = (
            wide * lax.rsqrt(spread + NORM_EPS) * gain[...]
        ).astype(BF16)
    share = q_local // kv_local
    rows = normed.shape[0]
    rows_dev = rows // blocks
    lane = lax.broadcasted_iota(jnp.int32, (rows, LANES), 1)
    low_half = lane % HS < HS // 2
    low_head = lane < HS

    def turned(values, cosine, sine):
        swapped = jnp.where(
            low_half, pltpu.roll(values, LANES - HS // 2, 1), pltpu.roll(values, HS // 2, 1)
        )
        return values * cosine + swapped * sine

    cosine = cos[...]
    sine = sin[...]
    keyval = jnp.dot(normed[...], wkv[...], preferred_element_type=F32)
    cosine_kv = jnp.where(low_head, cosine, 1.0)
    sine_kv = jnp.where(low_head, sine, 0.0)
    for g in range(kv_local):
        here = slice(g * LANES, (g + 1) * LANES)
        kv_out[:, here] = turned(keyval[:, here], cosine_kv, sine_kv).astype(BF16)
    queries = jnp.dot(normed[...], wq[...], preferred_element_type=F32)
    for pair in range(queries.shape[1] // LANES):
        both = turned(queries[:, pair * LANES : (pair + 1) * LANES], cosine, sine) * HS ** (-0.5)
        for odd in range(2):
            head = 2 * pair + odd
            if head >= q_local:
                continue
            alone = pltpu.roll(both, HS, 1) if odd else both
            alone = jnp.where(low_head, alone, 0.0).astype(BF16)
            group, slot = head // share, head % share
            for j in range(blocks):
                q_outs[j][group, slot * rows_dev : (slot + 1) * rows_dev, :] = alone[
                    j * rows_dev : (j + 1) * rows_dev
                ]


def project(pieces, gain, w_query, w_keyval, cos, sin, kv_local, q_local):
    blocks = len(pieces)
    rows_dev, width = pieces[0].shape
    share = q_local // kv_local
    outs = pl.pallas_call(
        functools.partial(project_kernel, blocks, kv_local, q_local),
        out_shape=[jax.ShapeDtypeStruct((kv_local, share * rows_dev, LANES), BF16)] * blocks
        + [jax.ShapeDtypeStruct((blocks * rows_dev, kv_local * LANES), BF16)],
        in_specs=[vmem()] * (blocks + 5),
        out_specs=[vmem()] * (blocks + 1),
        scratch_shapes=[pltpu.VMEM((blocks * rows_dev, width), BF16)],
        compiler_params=params(),
        cost_estimate=pl.CostEstimate(
            flops=4 * 10**9, bytes_accessed=4 * 10**6, transcendentals=blocks * rows_dev
        ),
        name="norm_project_rotate",
    )(*pieces, gain, w_query, w_keyval, cos.reshape(-1, LANES), sin.reshape(-1, LANES))
    return list(outs[:-1]), outs[-1]


def attend_kernel(block, near_parts, slab_spec, q_local, *refs):
    near_list, reach, read, slab_list, slab_count, fill, slab_id, place = refs[:8]
    info, query = refs[8:10]
    near_refs = refs[10 : 10 + near_parts]
    slab_refs = refs[10 + near_parts : -16]
    w_ref, out = refs[-16:-14]
    near, far, scores, peak, total, accum, begin, owner, heads, mixed, w_all = refs[-14:-3]
    near_sems, slab_sems, w_sem = refs[-3:]
    parts = near_list.shape[0]
    kv_local, stack, _ = query.shape
    rows_dev = info.shape[0]
    share = stack // rows_dev
    cuts = PREFIX // LANES
    window = parts + 1
    wide = (stack, LANES)
    lane = lax.broadcasted_iota(jnp.int32, (1, LANES), 1)

    def lanes(ref, g, rows, start=0):
        return ref.at[pl.ds(start, rows), pl.ds(g * LANES, LANES)]

    copies = []
    base = 0
    for i, ref in enumerate(near_refs):
        for g in range(kv_local):
            copies.append(
                pltpu.make_async_copy(
                    lanes(ref, g, ref.shape[0]),
                    near.at[g, pl.ds(base, ref.shape[0])],
                    near_sems.at[i, g],
                )
            )
        base += ref.shape[0]

    def each_slab(act):
        for i, [(array, start, _)] in enumerate(slab_spec):
            @pl.when(read[block, i] != 0)
            def _(i=i, array=array, start=start):
                for g in range(kv_local):
                    act(
                        pltpu.make_async_copy(
                            lanes(slab_refs[array], g, PREFIX, start),
                            far.at[g, pl.ds(i * PREFIX, PREFIX)],
                            slab_sems.at[i, g],
                        )
                    )

    w_copy = pltpu.make_async_copy(w_ref, w_all, w_sem)
    for copy in copies:
        copy.start()
    each_slab(lambda copy: copy.start())
    w_copy.start()
    for ref, column in ((owner, 0), (begin, 1)):
        tall = jnp.concatenate([info[:, column : column + 1]] * share, axis=0)
        ref[...] = jnp.broadcast_to(tall, wide)
    row = lax.broadcasted_iota(jnp.int32, wide, 0)
    order = row - lax.div(row, rows_dev) * rows_dev
    for copy in copies:
        copy.wait()

    def rows_near(g, back):
        unit = near_list[block, back]
        return near[g, pl.ds(pl.multiple_of(unit * rows_dev, rows_dev), rows_dev), :]

    def rows_window(g, backs):
        return jnp.concatenate([rows_near(g, back) for back in backs], axis=0)

    def rows_far(g, slab):
        return far[g, pl.ds(pl.multiple_of(slab * PREFIX, PREFIX), PREFIX), :]

    def score(g, rows):
        return lax.dot_general(
            query[g], rows, (((1,), (1,)), ((), ())), preferred_element_type=F32
        )

    def near_scores(backs, opening):
        for g in range(kv_local):
            every = score(g, rows_window(g, backs))
            top = None if opening else peak[g]
            for at, back in enumerate(backs):
                there = place[near_list[block, back]] + lane
                seen = there >= begin[...]
                if back == 0:
                    seen = seen & (lane <= order)
                here = every[:, at * LANES : (at + 1) * LANES]
                here = jnp.where(seen, here, NEG_FILL)
                scores[g, back] = here
                top = here if top is None else jnp.maximum(top, here)
            peak[g] = top

    def far_scores(slab):
        mine = owner[...] == slab_id[slab]
        for g in range(kv_local):
            every = score(g, rows_far(g, slab))
            top = None
            for c in range(cuts):
                here = every[:, c * LANES : (c + 1) * LANES]
                if (c + 1) * LANES > PREFIX // 2:
                    here = jnp.where(lane + c * LANES < fill[slab], here, NEG_FILL)
                scores[g, window + slab * cuts + c] = here
                top = here if top is None else jnp.maximum(top, here)
            old = peak[g]
            peak[g] = jnp.where(mine, jnp.maximum(old, top), old)

    def near_values(backs, opening):
        for g in range(kv_local):
            weights = [jnp.exp(scores[g, back] - peak[g]) for back in backs]
            packed = jnp.concatenate([part.astype(BF16) for part in weights], axis=1)
            summed = functools.reduce(jnp.add, weights)
            product = jnp.dot(packed, rows_window(g, backs), preferred_element_type=F32)
            if opening:
                total[g] = summed
                accum[g] = product
            else:
                total[g] += summed
                accum[g] += product

    def far_values(slab):
        mine = owner[...] == slab_id[slab]
        for g in range(kv_local):
            shift = jnp.where(mine, peak[g], -NEG_FILL)
            weights = [
                jnp.exp(scores[g, window + slab * cuts + c] - shift) for c in range(cuts)
            ]
            packed = jnp.concatenate([part.astype(BF16) for part in weights], axis=1)
            total[g] += functools.reduce(jnp.add, weights)
            accum[g] += jnp.dot(packed, rows_far(g, slab), preferred_element_type=F32)

    def sweep(near_body, far_body, between=None):
        near_body((0, 1), True)

        @pl.when(reach[block] != 0)
        def _():
            near_body(tuple(range(2, window)), False)

        if between is not None:
            between()

        @pl.loop(0, slab_count[block])
        def _(turn):
            far_body(slab_list[block, turn])

    sweep(near_scores, far_scores, lambda: each_slab(lambda copy: copy.wait()))
    for g in range(kv_local):
        peak[g] = jnp.broadcast_to(jnp.max(peak[g], axis=1, keepdims=True), wide)
    sweep(near_values, far_values)
    for g in range(kv_local):
        result = accum[g] / jnp.sum(total[g], axis=1, keepdims=True)
        for slot in range(share):
            heads[g * share + slot] = result[slot * rows_dev : (slot + 1) * rows_dev]

    low = lax.broadcasted_iota(jnp.int32, (rows_dev, LANES), 1) < HS
    for pair in range((q_local + 1) // 2):
        left = pltpu.roll(heads[2 * pair], HS, 1)
        here = slice(pair * LANES, (pair + 1) * LANES)
        if 2 * pair + 1 < q_local:
            mixed[:, here] = jnp.where(low, left, heads[2 * pair + 1]).astype(BF16)
        else:
            mixed[:, pair * LANES :] = left[:, :HS].astype(BF16)
    w_copy.wait()
    out[...] = jnp.dot(mixed[...], w_all[...], preferred_element_type=F32).astype(out.dtype)


def attend(block, tables, info, query, near, slabs, w_out, q_local, held_as):
    parts = info.shape[0]
    kv_local, stack, _ = query.shape
    rows_dev = info.shape[1]
    units = parts + 1 + len(slabs) * (PREFIX // LANES)
    wide = (stack, LANES)
    arrays, slab_spec = flatten(slabs)
    return pl.pallas_call(
        functools.partial(attend_kernel, block, len(near), slab_spec, q_local),
        out_shape=jax.ShapeDtypeStruct((rows_dev, w_out.shape[1]), held_as),
        in_specs=[SMEM] * 8 + [vmem()] * 2 + [ANY] * (len(near) + len(arrays) + 1),
        out_specs=vmem(),
        scratch_shapes=[
            pltpu.VMEM((kv_local, 2 * parts * rows_dev, LANES), BF16),
            pltpu.VMEM((kv_local, len(slabs) * PREFIX, LANES), BF16),
            pltpu.VMEM((kv_local, units) + wide, F32),
            pltpu.VMEM((kv_local,) + wide, F32),
            pltpu.VMEM((kv_local,) + wide, F32),
            pltpu.VMEM((kv_local,) + wide, F32),
            pltpu.VMEM(wide, jnp.int32),
            pltpu.VMEM(wide, jnp.int32),
            pltpu.VMEM((q_local, rows_dev, LANES), F32),
            pltpu.VMEM((rows_dev, q_local * HS), BF16),
            pltpu.VMEM(w_out.shape, BF16),
            pltpu.SemaphoreType.DMA((len(near), kv_local)),
            pltpu.SemaphoreType.DMA((len(slabs), kv_local)),
            pltpu.SemaphoreType.DMA,
        ],
        compiler_params=params(),
        cost_estimate=pl.CostEstimate(
            flops=8 * 10**9, bytes_accessed=4 * 10**6, transcendentals=10**6
        ),
        name="attend",
    )(
        tables["near_list"],
        tables["reach"],
        tables["read"],
        tables["slab_list"],
        tables["slab_count"],
        tables["fill"],
        tables["slab_id"],
        tables["place"],
        info[block],
        query,
        *near,
        *arrays,
        w_out,
    )


def hidden_kernel(tokens, gain, own, *refs):
    others = refs[:-2]
    hidden, expert_in = refs[-2:]
    total = tokens[...].astype(F32) + own[...]
    for other in others:
        total += other[...].astype(F32)
    hidden[...] = total
    spread = jnp.mean(total * total, axis=-1, keepdims=True)
    expert_in[...] = (total * lax.rsqrt(spread + NORM_EPS) * gain[...]).astype(BF16)


def add_and_norm(tokens, gain, own, others):
    return pl.pallas_call(
        hidden_kernel,
        out_shape=(
            jax.ShapeDtypeStruct(tokens.shape, F32),
            jax.ShapeDtypeStruct(tokens.shape, BF16),
        ),
        in_specs=[vmem()] * (3 + len(others)),
        out_specs=(vmem(), vmem()),
        compiler_params=params(),
        cost_estimate=pl.CostEstimate(
            flops=10**9, bytes_accessed=16 * tokens.size, transcendentals=tokens.shape[0]
        ),
        name="add_and_norm",
    )(tokens, gain, own, *others)


def expert_kernel(spec, rows, slot_row, gate_row, slot_col, *refs):
    count = len(spec)
    many = len(refs) - 15
    x_refs = refs[:many]
    wg_ref, wu_ref, wd_ref, near, far, last = refs[many : many + 6]
    x_all, wg, wu, wd, picked, answered, inner, x_sem, w_sem = refs[many + 6 :]
    exp_local = wg.shape[0]
    width = x_all.shape[1]
    span = 2 * rows
    slots = 2 * CAP
    pairs = count // 2
    chunk = 512

    x_copies = []
    base = 0
    for array, there, many_rows in [piece for pieces in spec for piece in pieces]:
        x_copies.append(
            pltpu.make_async_copy(
                x_refs[array].at[pl.ds(there, many_rows)],
                x_all.at[pl.ds(base, many_rows)],
                x_sem.at[len(x_copies)],
            )
        )
        base += many_rows
    for copy in x_copies:
        copy.start()

    def w_copies(e):
        return [
            pltpu.make_async_copy(source.at[e], target.at[e], w_sem.at[e, i])
            for i, (source, target) in enumerate(((wg_ref, wg), (wu_ref, wu), (wd_ref, wd)))
        ]

    for e in range(exp_local):
        for copy in w_copies(e):
            copy.start()
    for copy in x_copies:
        copy.wait()

    slot_iota = lax.broadcasted_iota(jnp.int32, (slots, span), 0)

    def pair_hits(e, b):
        there = slice(b * span, (b + 1) * span)
        return slot_iota == slot_row[pl.ds(e, 1), there]

    for b in range(pairs):
        hits = [jnp.where(pair_hits(e, b), 1.0, 0.0).astype(BF16) for e in range(exp_local)]
        chooser = jnp.concatenate(hits, axis=0)
        for c in range(0, width, chunk):
            found = jnp.dot(
                chooser,
                x_all[b * span : (b + 1) * span, c : c + chunk],
                preferred_element_type=F32,
            ).astype(BF16)
            for e in range(exp_local):
                picked[e, b * slots : (b + 1) * slots, c : c + chunk] = found[
                    e * slots : (e + 1) * slots
                ]

    @pl.loop(0, exp_local)
    def _(e):
        for copy in w_copies(e):
            copy.wait()
        rows_in = picked[e]
        for c in range(0, inner.shape[1], 256):
            gate = jnp.dot(rows_in, wg[e, :, c : c + 256], preferred_element_type=F32)
            up = jnp.dot(rows_in, wu[e, :, c : c + 256], preferred_element_type=F32)
            inner[:, c : c + 256] = (gate / (1.0 + jnp.exp(-gate)) * up).astype(BF16)
        scale = jnp.concatenate(
            [
                jnp.sum(
                    jnp.where(
                        pair_hits(e, b), gate_row[pl.ds(e, 1), b * span : (b + 1) * span], 0.0
                    ),
                    axis=1,
                    keepdims=True,
                )
                for b in range(pairs)
            ],
            axis=0,
        )
        for c in range(0, width, chunk):
            answer = jnp.dot(inner[...], wd[e, :, c : c + chunk], preferred_element_type=F32)
            answer = (answer * scale).astype(BF16)
            for b in range(pairs):
                first = pl.multiple_of(e * slots, slots)
                answered[b, pl.ds(first, slots), c : c + chunk] = answer[
                    b * slots : (b + 1) * slots
                ]

    lane = lax.broadcasted_iota(jnp.int32, (span, slots), 1)
    for b in range(pairs):
        there = slice(b * span, (b + 1) * span)
        spreader = jnp.concatenate(
            [
                jnp.where(lane == slot_col[there, e : e + 1], 1.0, 0.0).astype(BF16)
                for e in range(exp_local)
            ],
            axis=1,
        )
        for c in range(0, width, chunk):
            sums = jnp.dot(
                spreader, answered[b, :, c : c + chunk], preferred_element_type=F32
            ).astype(BF16)
            base = (b - pairs // 2) * span
            if b < pairs // 2:
                near[b * span : (b + 1) * span, c : c + chunk] = sums
            elif b < pairs - 1:
                far[base : base + span, c : c + chunk] = sums
            else:
                far[base : base + rows, c : c + chunk] = sums[:rows]
                last[:, c : c + chunk] = sums[rows:]


def experts(blocks, slot_row, gate_row, slot_col, w_gate, w_up, w_down):
    count = len(blocks)
    pieces, spec = flatten(blocks)
    parts = sum(len(one) for one in spec)
    rows, width = blocks[0][0][2], pieces[0].shape[1]
    exp_local, _, hidden = w_gate.shape
    pairs = count // 2
    slots = 2 * CAP
    work = exp_local * pairs * slots
    return pl.pallas_call(
        functools.partial(expert_kernel, spec, rows),
        out_shape=tuple(
            jax.ShapeDtypeStruct((many * rows, width), BF16)
            for many in (count // 2, count // 2 - 1, 1)
        ),
        in_specs=[vmem()] * 3 + [ANY] * (len(pieces) + 3),
        out_specs=(vmem(), vmem(), vmem()),
        scratch_shapes=[
            pltpu.VMEM((count * rows, width), BF16),
            pltpu.VMEM(w_gate.shape, BF16),
            pltpu.VMEM(w_up.shape, BF16),
            pltpu.VMEM(w_down.shape, BF16),
            pltpu.VMEM((exp_local, pairs * slots, width), BF16),
            pltpu.VMEM((pairs, exp_local * slots, width), BF16),
            pltpu.VMEM((pairs * slots, hidden), BF16),
            pltpu.SemaphoreType.DMA((parts,)),
            pltpu.SemaphoreType.DMA((exp_local, 3)),
        ],
        compiler_params=params(),
        cost_estimate=pl.CostEstimate(
            flops=2 * work * width * (3 * hidden + 4 * rows),
            bytes_accessed=2 * (3 * w_gate.size + 2 * count * rows * width),
            transcendentals=work * hidden,
        ),
        name="experts",
    )(slot_row, gate_row, slot_col, *pieces, w_gate, w_up, w_down)


def packed_routes(routes, route_gates, lanes):
    parts = [routes.T.astype(BF16)]
    rest = route_gates.T
    for _ in range(3):
        term = lax.reduce_precision(rest, 8, 7)
        parts.append(term.astype(BF16))
        rest = rest - term
    per = len(parts) * LANES // lanes
    return jnp.concatenate(
        [jnp.concatenate(parts[i : i + per], axis=0) for i in range(0, len(parts), per)], axis=1
    )


def route_kernel(spec, first_expert, *refs):
    count = len(spec)
    sources = refs[:-5]
    slot_row, gate_row, slot_col, packed, sems = refs[-5:]
    exp_local = slot_row.shape[0]
    tall = packed.shape[1]
    copies = [
        pltpu.make_async_copy(
            sources[array].at[pl.ds(there + rows - tall, tall), pl.ds(0, packed.shape[2])],
            packed.at[k],
            sems.at[k],
        )
        for k, (array, there, rows) in enumerate(pieces[-1] for pieces in spec)
    ]
    for copy in copies:
        copy.start()
    for copy in copies:
        copy.wait()
    here = lax.broadcasted_iota(jnp.int32, (LANES, LANES), 1)
    there = lax.broadcasted_iota(jnp.int32, (LANES, LANES), 0)
    earlier = jnp.where(there < here, 1.0, 0.0).astype(BF16)
    choices = tall * packed.shape[2] // (4 * LANES)
    for k in range(count):
        block = packed[k].astype(F32)
        parts = [
            block[r : r + choices, c : c + LANES]
            for c in range(0, packed.shape[2], LANES)
            for r in range(0, tall, choices)
        ]
        named = parts[0]
        gates = parts[1] + parts[2] + parts[3]
        hits, shares = [], []
        for e in range(exp_local):
            match = named == (first_expert[0] + e).astype(F32)
            hits.append(jnp.max(jnp.where(match, 1.0, 0.0), axis=0, keepdims=True))
            shares.append(jnp.sum(jnp.where(match, gates, 0.0), axis=0, keepdims=True))
        hits += [jnp.zeros((1, LANES), F32)] * (8 - exp_local)
        hit = jnp.concatenate(hits, axis=0)
        rank = jnp.dot(hit.astype(BF16), earlier, preferred_element_type=F32)
        slot = jnp.where(hit > 0.0, rank + float(k % 2 * CAP), -1.0)
        lanes = slice(k * LANES, (k + 1) * LANES)
        slot_row[:, lanes] = slot[:exp_local].astype(jnp.int32)
        gate_row[:, lanes] = jnp.concatenate(shares, axis=0)
        slot_col[lanes, :] = slot.T.astype(jnp.int32)


def route_tables(sources, tall, lanes, first_expert, exp_local):
    count = len(sources)
    sources, spec = flatten(sources)
    tokens = count * LANES
    return pl.pallas_call(
        functools.partial(route_kernel, spec),
        out_shape=(
            jax.ShapeDtypeStruct((exp_local, tokens), jnp.int32),
            jax.ShapeDtypeStruct((exp_local, tokens), F32),
            jax.ShapeDtypeStruct((tokens, 8), jnp.int32),
        ),
        in_specs=[SMEM] + [ANY] * len(sources),
        out_specs=(vmem(), vmem(), vmem()),
        scratch_shapes=[
            pltpu.VMEM((count, tall, lanes), BF16),
            pltpu.SemaphoreType.DMA((count,)),
        ],
        compiler_params=params(),
        cost_estimate=pl.CostEstimate(
            flops=3 * 10**9, bytes_accessed=10**6, transcendentals=0
        ),
        name="route_tables",
    )(first_expert, *sources)


def local(
    tokens,
    segments,
    group_ids,
    prefix_owner,
    slab_fill,
    prefix_cache,
    attn_gain,
    w_query,
    w_keyval,
    w_out,
    ffn_gain,
    routes,
    route_gates,
    w_gate,
    w_up,
    w_down,
):
    tok_count = lax.axis_size("tok")
    groups = lax.axis_size("head")
    me_tok = lax.axis_index("tok")
    me_head = lax.axis_index("head")
    rows_dev, width = tokens.shape
    row_len = rows_dev * groups
    row_first = me_tok * row_len
    kv_local = w_keyval.shape[1] // (2 * HS)
    q_local = w_query.shape[1] // HS
    origins = plane_origins()

    turns = [tokens]
    for _ in range(groups // 2):
        turns.append(next_turn(turns[-1], "head"))

    steps = jnp.arange(groups, dtype=jnp.int32)
    block_of = (me_head - steps) % groups
    token_id = row_first + block_of[:, None] * rows_dev + jnp.arange(rows_dev, dtype=jnp.int32)
    row_segs = lax.dynamic_slice_in_dim(segments, row_first, row_len, 0).reshape(groups, rows_dev)
    segs = jnp.sum(
        jnp.where((block_of[:, None] == steps[None, :])[:, :, None], row_segs[None], 0), axis=1
    )
    requests = jnp.arange(group_ids.shape[0], dtype=jnp.int32)
    starts = jnp.sum((segments[None, :] < requests[:, None]).astype(jnp.int32), axis=1)
    begin = lookup(starts, segs)
    slab = lookup(lookup(prefix_owner, group_ids), segs)
    fill = lookup(slab_fill, slab)
    position = fill + token_id - begin
    steps_idx = jnp.arange(HS // 2, dtype=F32)
    inverse = jnp.exp(steps_idx * (-2.0 * jnp.log(10000.0) / HS))
    angles = position.astype(F32)[:, :, None] * inverse
    cosine = jnp.cos(angles)
    sine = jnp.sin(angles)
    cos = jnp.concatenate([cosine] * 4, axis=2)
    sin = jnp.concatenate([-sine, sine, -sine, sine], axis=2)
    info = jnp.stack([slab, begin, token_id, token_id], axis=2)
    place = token_id[:, 0]
    backs = jnp.arange(groups + 1, dtype=jnp.int32)
    read = jnp.any(slab[:, :, None] == origins, axis=1).astype(jnp.int32)
    spot = jnp.arange(read.shape[1], dtype=jnp.int32)
    rank = jnp.sum(jnp.where(spot[:, None] < spot[None, :], read[:, :, None], 0), axis=1)
    tables = {
        "near_list": (steps[:, None] + backs[None, :]) % groups
        + jnp.where(block_of[:, None] >= backs[None, :], groups, 0),
        "reach": (begin[:, 0] < place - rows_dev).astype(jnp.int32),
        "read": read,
        "slab_list": jnp.sum(
            jnp.where(
                (rank[:, :, None] == spot[None, None, :]) & (read[:, :, None] != 0),
                spot[None, :, None],
                0,
            ),
            axis=1,
        ),
        "slab_count": jnp.sum(read, axis=1),
        "fill": lookup(slab_fill, origins),
        "slab_id": origins,
        "place": jnp.concatenate([place - row_len, place]),
    }

    missing = -w_query.shape[1] % LANES
    if missing:
        w_query = jnp.pad(w_query, ((0, 0), (0, missing)))
    queries, own, prev = [], [], []
    for some in (slice(0, groups // 2), slice(groups // 2, groups)):
        while len(turns) < some.stop:
            turns.append(next_turn(after(turns[-1], own[0]), "head"))
        query, keyval = project(
            turns[some],
            attn_gain[None, :],
            w_query,
            w_keyval,
            cos[some],
            sin[some],
            kv_local,
            q_local,
        )
        queries += query
        own.append(keyval)
        prev.append(lax.ppermute(keyval, "tok", [(i, i + 1) for i in range(tok_count - 1)]))

    def exchanged(block, j):
        return lax.ppermute(block, "head", [(i, (i - j) % groups) for i in range(groups)])

    lanes = prefix_cache.shape[1]
    packed = packed_routes(routes, route_gates, lanes)
    cached = plane_gather(
        jnp.concatenate([prefix_cache, packed], axis=0), False, True, [own[0], None, turns[-1]]
    )

    near = prev + own

    def term(j, held_as):
        return attend(j, tables, info, queries[j], near, cached, w_out, q_local, held_as)

    down = groups // 2
    up = groups - 1 - down
    lower = upper = None
    for turn in range(down):
        here = term(down - turn, BF16)
        if lower is not None:
            here = (here.astype(F32) + lower.astype(F32)).astype(BF16)
        lower = exchanged(here, 1)
        if turn < up:
            here = term(groups - up + turn, BF16)
            if upper is not None:
                here = (here.astype(F32) + upper.astype(F32)).astype(BF16)
            upper = exchanged(here, groups - 1)
    terms = [lower] if upper is None else [lower, upper]
    own_term = term(0, F32)
    hidden, expert_in = add_and_norm(tokens, ffn_gain[None, :], own_term, terms)

    exp_local = w_gate.shape[0]
    route = route_tables(
        cached,
        packed.shape[0],
        lanes,
        (me_tok * exp_local).astype(jnp.int32).reshape(1),
        exp_local,
    )
    blocks = plane_gather(expert_in, True, False, [None, route[0], None])
    near, far, last = experts(blocks, *route, w_gate, w_up, w_down)
    return (hidden + plane_sum(near, far, last, rows_dev)).astype(BF16)


def solution(mesh):
    return jax.shard_map(
        local,
        mesh=mesh,
        in_specs=(
            P(("tok", "head"), None),
            P(),
            P(),
            P(),
            P(),
            P("tok", "head"),
            P(),
            P(None, "head"),
            P(None, "head"),
            P("head", None),
            P(),
            P(("tok", "head"), None),
            P(("tok", "head"), None),
            P("tok", None, None),
            P("tok", None, None),
            P("tok", None, None),
        ),
        out_specs=P(("tok", "head"), None),
        check_vma=False,
    )
```

```python
import functools

import jax
import jax.numpy as jnp
from jax import lax
from jax.experimental import pallas as pl
from jax.experimental.pallas import tpu as pltpu
from jax.sharding import PartitionSpec as P

HS = 64
CAP = 64
PREFIX = 512
LANES = 128
NEG_FILL = -1e30
NORM_EPS = 1e-06
F32 = jnp.float32
BF16 = jnp.bfloat16
VMEM_BYTES = 56 * 1024 * 1024


def vmem(*shape):
    return pl.BlockSpec(memory_space=pltpu.VMEM)


ANY = pl.BlockSpec(memory_space=pl.ANY)
SMEM = pl.BlockSpec(memory_space=pltpu.SMEM)


def params(**more):
    return pltpu.CompilerParams(vmem_limit_bytes=VMEM_BYTES, **more)


def lookup(table, index):
    entries = jnp.arange(table.shape[0], dtype=jnp.int32)
    return jnp.sum(jnp.where(index[..., None] == entries, table, 0), axis=-1)


def next_turn(block, axis):
    count = lax.axis_size(axis)
    return lax.ppermute(block, axis, [(i, (i + 1) % count) for i in range(count)])


def cube_routes():
    first = [(t, t ^ (2 if t & 1 else 4)) for t in range(8)]
    second = [(t, t ^ (4 if t & 1 else 2)) for t in range(8)]
    partner = [(t, t ^ 1) for t in range(8)]
    return first, second, partner


def plane_origins():
    count = lax.axis_size("tok")
    if count != 8:
        return jnp.arange(count, dtype=jnp.int32)
    me = lax.axis_index("tok")
    one = jnp.where(me % 2 == 0, 4, 2)
    two = 6 - one
    other = me ^ 1
    return jnp.stack(
        [me, me ^ one, me ^ two, me ^ 6, other, other ^ two, other ^ one, other ^ 6]
    ).astype(jnp.int32)


def to_neighbours(block):
    if lax.axis_size("tok") != 8:
        return []
    first, second, _ = cube_routes()
    return [lax.ppermute(block, "tok", first), lax.ppermute(block, "tok", second)]


def to_plane(block, neighbours, tie):
    count = lax.axis_size("tok")
    rows = block.shape[0]
    if count != 8:
        whole = lax.all_gather(block, "tok", axis=0, tiled=True)
        return [[(whole, i * rows, rows)] for i in range(count)]
    _, second, partner = cube_routes()
    across = lax.ppermute(neighbours[0], "tok", second)
    every = jnp.concatenate(after([block, *neighbours, across], tie), axis=0)
    return [
        [(side, i * rows, rows)]
        for side in (every, lax.ppermute(every, "tok", partner))
        for i in range(4)
    ]


def flatten(blocks):
    arrays, spec = [], []
    for pieces in blocks:
        here = []
        for array, first, rows in pieces:
            known = [i for i, other in enumerate(arrays) if other is array]
            if not known:
                known = [len(arrays)]
                arrays.append(array)
            here.append((known[0], first, rows))
        spec.append(here)
    return arrays, spec


def row_ranges(pieces, first, count):
    base = 0
    for array, start, rows in pieces:
        low, high = max(first, base), min(first + count, base + rows)
        if low < high:
            yield array, start + low - base, low - first, high - low
        base += rows


def after(value, tie):
    return value if tie is None else lax.optimization_barrier((value, tie))[0]


def plane_sum(near, far, last, rows):
    first, second, partner = cube_routes()
    half = rows // 2
    got_last = lax.ppermute(last, "tok", partner)
    got = lax.ppermute(far, "tok", partner)
    three = (near[3 * rows :].astype(F32) + got_last.astype(F32)).astype(BF16)
    across_upper = lax.ppermute(three[:half], "tok", second)
    across_lower = lax.ppermute(three[half:], "tok", first)
    near, got = after((near, got), (across_upper, across_lower))

    def pair(block):
        here = slice(block * rows, (block + 1) * rows)
        return near[here].astype(F32) + got[here].astype(F32)

    nothing = jnp.zeros(across_upper.shape, F32)
    add_upper = jnp.concatenate([across_upper.astype(F32), nothing], axis=0)
    add_lower = jnp.concatenate([nothing, across_lower.astype(F32)], axis=0)
    along = lax.ppermute((pair(1) + add_upper).astype(BF16), "tok", first)
    beside = lax.ppermute((pair(2) + add_lower).astype(BF16), "tok", second)
    return pair(0) + beside.astype(F32) + along.astype(F32)


def project_kernel(blocks, kv_local, q_local, *refs):
    pieces = refs[: 2 * blocks]
    gain, wq, wkv, cos, sin = refs[2 * blocks : 2 * blocks + 5]
    q_outs = refs[2 * blocks + 5 : 3 * blocks + 5]
    kv_out, normed = refs[3 * blocks + 5 :]
    half = pieces[0].shape[0]
    for i, piece in enumerate(pieces):
        wide = piece[...].astype(F32)
        spread = jnp.mean(wide * wide, axis=-1, keepdims=True)
        normed[i * half : (i + 1) * half, :] = (
            wide * lax.rsqrt(spread + NORM_EPS) * gain[...]
        ).astype(BF16)
    share = q_local // kv_local
    rows = normed.shape[0]
    rows_dev = rows // blocks
    lane = lax.broadcasted_iota(jnp.int32, (rows, LANES), 1)
    low_half = lane % HS < HS // 2
    low_head = lane < HS

    def turned(values, cosine, sine):
        swapped = jnp.where(
            low_half, pltpu.roll(values, LANES - HS // 2, 1), pltpu.roll(values, HS // 2, 1)
        )
        return values * cosine + swapped * sine

    cosine = cos[...]
    sine = sin[...]
    keyval = jnp.dot(normed[...], wkv[...], preferred_element_type=F32)
    cosine_kv = jnp.where(low_head, cosine, 1.0)
    sine_kv = jnp.where(low_head, sine, 0.0)
    for g in range(kv_local):
        here = slice(g * LANES, (g + 1) * LANES)
        kv_out[:, here] = turned(keyval[:, here], cosine_kv, sine_kv).astype(BF16)
    queries = jnp.dot(normed[...], wq[...], preferred_element_type=F32)
    for pair in range(queries.shape[1] // LANES):
        both = turned(queries[:, pair * LANES : (pair + 1) * LANES], cosine, sine) * HS ** (-0.5)
        for odd in range(2):
            head = 2 * pair + odd
            if head >= q_local:
                continue
            alone = pltpu.roll(both, HS, 1) if odd else both
            alone = jnp.where(low_head, alone, 0.0).astype(BF16)
            group, slot = head // share, head % share
            for j in range(blocks):
                q_outs[j][group, slot * rows_dev : (slot + 1) * rows_dev, :] = alone[
                    j * rows_dev : (j + 1) * rows_dev
                ]


def project(pieces, gain, w_query, w_keyval, cos, sin, kv_local, q_local):
    blocks = len(pieces) // 2
    rows_dev, width = 2 * pieces[0].shape[0], pieces[0].shape[1]
    share = q_local // kv_local
    outs = pl.pallas_call(
        functools.partial(project_kernel, blocks, kv_local, q_local),
        out_shape=[jax.ShapeDtypeStruct((kv_local, share * rows_dev, LANES), BF16)] * blocks
        + [jax.ShapeDtypeStruct((blocks * rows_dev, kv_local * LANES), BF16)],
        in_specs=[vmem()] * (2 * blocks + 5),
        out_specs=[vmem()] * (blocks + 1),
        scratch_shapes=[pltpu.VMEM((blocks * rows_dev, width), BF16)],
        compiler_params=params(),
        cost_estimate=pl.CostEstimate(
            flops=4 * 10**9, bytes_accessed=4 * 10**6, transcendentals=blocks * rows_dev
        ),
        name="norm_project_rotate",
    )(*pieces, gain, w_query, w_keyval, cos.reshape(-1, LANES), sin.reshape(-1, LANES))
    return list(outs[:-1]), outs[-1]


def attend_kernel(block, near_parts, slab_spec, q_local, *refs):
    near_list, reach, read, slab_list, slab_count, fill, slab_id, place = refs[:8]
    info, query = refs[8:10]
    near_refs = refs[10 : 10 + near_parts]
    slab_refs = refs[10 + near_parts : -16]
    w_ref, out = refs[-16:-14]
    near, far, scores, peak, total, accum, begin, owner, heads, mixed, w_all = refs[-14:-3]
    near_sems, slab_sems, w_sem = refs[-3:]
    parts = near_list.shape[0]
    kv_local, stack, _ = query.shape
    rows_dev = info.shape[0]
    share = stack // rows_dev
    cuts = PREFIX // LANES
    window = parts + 1
    wide = (stack, LANES)
    lane = lax.broadcasted_iota(jnp.int32, (1, LANES), 1)

    def lanes(ref, g, rows, start=0):
        return ref.at[pl.ds(start, rows), pl.ds(g * LANES, LANES)]

    copies = []
    base = 0
    for i, ref in enumerate(near_refs):
        for g in range(kv_local):
            copies.append(
                pltpu.make_async_copy(
                    lanes(ref, g, ref.shape[0]),
                    near.at[g, pl.ds(base, ref.shape[0])],
                    near_sems.at[i, g],
                )
            )
        base += ref.shape[0]

    def each_slab(act):
        for i, [(array, start, _)] in enumerate(slab_spec):
            @pl.when(read[block, i] != 0)
            def _(i=i, array=array, start=start):
                for g in range(kv_local):
                    act(
                        pltpu.make_async_copy(
                            lanes(slab_refs[array], g, PREFIX, start),
                            far.at[g, pl.ds(i * PREFIX, PREFIX)],
                            slab_sems.at[i, g],
                        )
                    )

    w_copy = pltpu.make_async_copy(w_ref, w_all, w_sem)
    for copy in copies:
        copy.start()
    each_slab(lambda copy: copy.start())
    w_copy.start()
    for ref, column in ((owner, 0), (begin, 1)):
        tall = jnp.concatenate([info[:, column : column + 1]] * share, axis=0)
        ref[...] = jnp.broadcast_to(tall, wide)
    row = lax.broadcasted_iota(jnp.int32, wide, 0)
    order = row - lax.div(row, rows_dev) * rows_dev
    for copy in copies:
        copy.wait()

    def rows_near(g, back):
        unit = near_list[block, back]
        return near[g, pl.ds(pl.multiple_of(unit * rows_dev, rows_dev), rows_dev), :]

    def rows_window(g, backs):
        return jnp.concatenate([rows_near(g, back) for back in backs], axis=0)

    def rows_far(g, slab):
        return far[g, pl.ds(pl.multiple_of(slab * PREFIX, PREFIX), PREFIX), :]

    def score(g, rows):
        return lax.dot_general(
            query[g], rows, (((1,), (1,)), ((), ())), preferred_element_type=F32
        )

    def near_scores(backs, opening):
        for g in range(kv_local):
            every = score(g, rows_window(g, backs))
            top = None if opening else peak[g]
            for at, back in enumerate(backs):
                there = place[near_list[block, back]] + lane
                seen = there >= begin[...]
                if back == 0:
                    seen = seen & (lane <= order)
                here = every[:, at * LANES : (at + 1) * LANES]
                here = jnp.where(seen, here, NEG_FILL)
                scores[g, back] = here
                top = here if top is None else jnp.maximum(top, here)
            peak[g] = top

    def far_scores(slab):
        mine = owner[...] == slab_id[slab]
        for g in range(kv_local):
            every = score(g, rows_far(g, slab))
            top = None
            for c in range(cuts):
                here = every[:, c * LANES : (c + 1) * LANES]
                if (c + 1) * LANES > PREFIX // 2:
                    here = jnp.where(lane + c * LANES < fill[slab], here, NEG_FILL)
                scores[g, window + slab * cuts + c] = here
                top = here if top is None else jnp.maximum(top, here)
            old = peak[g]
            peak[g] = jnp.where(mine, jnp.maximum(old, top), old)

    def near_values(backs, opening):
        for g in range(kv_local):
            weights = [jnp.exp(scores[g, back] - peak[g]) for back in backs]
            packed = jnp.concatenate([part.astype(BF16) for part in weights], axis=1)
            summed = functools.reduce(jnp.add, weights)
            product = jnp.dot(packed, rows_window(g, backs), preferred_element_type=F32)
            if opening:
                total[g] = summed
                accum[g] = product
            else:
                total[g] += summed
                accum[g] += product

    def far_values(slab):
        mine = owner[...] == slab_id[slab]
        for g in range(kv_local):
            shift = jnp.where(mine, peak[g], -NEG_FILL)
            weights = [
                jnp.exp(scores[g, window + slab * cuts + c] - shift) for c in range(cuts)
            ]
            packed = jnp.concatenate([part.astype(BF16) for part in weights], axis=1)
            total[g] += functools.reduce(jnp.add, weights)
            accum[g] += jnp.dot(packed, rows_far(g, slab), preferred_element_type=F32)

    def sweep(near_body, far_body, between=None):
        near_body((0, 1), True)

        @pl.when(reach[block] != 0)
        def _():
            near_body(tuple(range(2, window)), False)

        if between is not None:
            between()

        @pl.loop(0, slab_count[block])
        def _(turn):
            far_body(slab_list[block, turn])

    sweep(near_scores, far_scores, lambda: each_slab(lambda copy: copy.wait()))
    for g in range(kv_local):
        peak[g] = jnp.broadcast_to(jnp.max(peak[g], axis=1, keepdims=True), wide)
    sweep(near_values, far_values)
    for g in range(kv_local):
        result = accum[g] / jnp.sum(total[g], axis=1, keepdims=True)
        for slot in range(share):
            heads[g * share + slot] = result[slot * rows_dev : (slot + 1) * rows_dev]

    low = lax.broadcasted_iota(jnp.int32, (rows_dev, LANES), 1) < HS
    for pair in range((q_local + 1) // 2):
        left = pltpu.roll(heads[2 * pair], HS, 1)
        here = slice(pair * LANES, (pair + 1) * LANES)
        if 2 * pair + 1 < q_local:
            mixed[:, here] = jnp.where(low, left, heads[2 * pair + 1]).astype(BF16)
        else:
            mixed[:, pair * LANES :] = left[:, :HS].astype(BF16)
    w_copy.wait()
    out[...] = jnp.dot(mixed[...], w_all[...], preferred_element_type=F32).astype(out.dtype)


def attend(block, tables, info, query, near, slabs, w_out, q_local, held_as):
    parts = info.shape[0]
    kv_local, stack, _ = query.shape
    rows_dev = info.shape[1]
    units = parts + 1 + len(slabs) * (PREFIX // LANES)
    wide = (stack, LANES)
    arrays, slab_spec = flatten(slabs)
    return pl.pallas_call(
        functools.partial(attend_kernel, block, len(near), slab_spec, q_local),
        out_shape=jax.ShapeDtypeStruct((rows_dev, w_out.shape[1]), held_as),
        in_specs=[SMEM] * 8 + [vmem()] * 2 + [ANY] * (len(near) + len(arrays) + 1),
        out_specs=vmem(),
        scratch_shapes=[
            pltpu.VMEM((kv_local, 2 * parts * rows_dev, LANES), BF16),
            pltpu.VMEM((kv_local, len(slabs) * PREFIX, LANES), BF16),
            pltpu.VMEM((kv_local, units) + wide, F32),
            pltpu.VMEM((kv_local,) + wide, F32),
            pltpu.VMEM((kv_local,) + wide, F32),
            pltpu.VMEM((kv_local,) + wide, F32),
            pltpu.VMEM(wide, jnp.int32),
            pltpu.VMEM(wide, jnp.int32),
            pltpu.VMEM((q_local, rows_dev, LANES), F32),
            pltpu.VMEM((rows_dev, q_local * HS), BF16),
            pltpu.VMEM(w_out.shape, BF16),
            pltpu.SemaphoreType.DMA((len(near), kv_local)),
            pltpu.SemaphoreType.DMA((len(slabs), kv_local)),
            pltpu.SemaphoreType.DMA,
        ],
        compiler_params=params(),
        cost_estimate=pl.CostEstimate(
            flops=8 * 10**9, bytes_accessed=4 * 10**6, transcendentals=10**6
        ),
        name="attend",
    )(
        tables["near_list"],
        tables["reach"],
        tables["read"],
        tables["slab_list"],
        tables["slab_count"],
        tables["fill"],
        tables["slab_id"],
        tables["place"],
        info[block],
        query,
        *near,
        *arrays,
        w_out,
    )


def hidden_kernel(tokens, gain, own, *refs):
    others = refs[:-2]
    hidden, expert_in = refs[-2:]
    total = tokens[...].astype(F32) + own[...]
    for other in others:
        total += other[...].astype(F32)
    hidden[...] = total
    spread = jnp.mean(total * total, axis=-1, keepdims=True)
    expert_in[...] = (total * lax.rsqrt(spread + NORM_EPS) * gain[...]).astype(BF16)


def add_and_norm(tokens, gain, own, others):
    return pl.pallas_call(
        hidden_kernel,
        out_shape=(
            jax.ShapeDtypeStruct(tokens.shape, F32),
            jax.ShapeDtypeStruct(tokens.shape, BF16),
        ),
        in_specs=[vmem()] * (3 + len(others)),
        out_specs=(vmem(), vmem()),
        compiler_params=params(),
        cost_estimate=pl.CostEstimate(
            flops=10**9, bytes_accessed=16 * tokens.size, transcendentals=tokens.shape[0]
        ),
        name="add_and_norm",
    )(tokens, gain, own, *others)


def expert_kernel(spec, rows, layout, slot_row, gate_row, slot_col, *refs):
    count = len(spec)
    x_refs = refs[: -12 - len(layout)]
    wg_ref, wu_ref, wd_ref = refs[-12 - len(layout) : -9 - len(layout)]
    outs = refs[-9 - len(layout) : -9]
    x_all, wg, wu, wd, picked, answered, inner, x_sem, w_sem = refs[-9:]
    targets = [(out, i) for out, many in zip(outs, layout) for i in range(many)]
    exp_local = wg.shape[0]
    width = x_all.shape[1]
    span = 2 * rows
    slots = 2 * CAP
    pairs = count // 2
    chunk = 512

    x_copies = []
    base = 0
    for array, there, many_rows in [piece for pieces in spec for piece in pieces]:
        x_copies.append(
            pltpu.make_async_copy(
                x_refs[array].at[pl.ds(there, many_rows)],
                x_all.at[pl.ds(base, many_rows)],
                x_sem.at[len(x_copies)],
            )
        )
        base += many_rows
    for copy in x_copies:
        copy.start()

    def w_copies(e):
        return [
            pltpu.make_async_copy(source.at[e], target.at[e], w_sem.at[e, i])
            for i, (source, target) in enumerate(((wg_ref, wg), (wu_ref, wu), (wd_ref, wd)))
        ]

    for e in range(exp_local):
        for copy in w_copies(e):
            copy.start()
    for copy in x_copies:
        copy.wait()

    slot_iota = lax.broadcasted_iota(jnp.int32, (slots, span), 0)

    def pair_hits(e, b):
        there = slice(b * span, (b + 1) * span)
        return slot_iota == slot_row[pl.ds(e, 1), there]

    for b in range(pairs):
        hits = [jnp.where(pair_hits(e, b), 1.0, 0.0).astype(BF16) for e in range(exp_local)]
        chooser = jnp.concatenate(hits, axis=0)
        for c in range(0, width, chunk):
            found = jnp.dot(
                chooser,
                x_all[b * span : (b + 1) * span, c : c + chunk],
                preferred_element_type=F32,
            ).astype(BF16)
            for e in range(exp_local):
                picked[e, b * slots : (b + 1) * slots, c : c + chunk] = found[
                    e * slots : (e + 1) * slots
                ]

    @pl.loop(0, exp_local)
    def _(e):
        for copy in w_copies(e):
            copy.wait()
        rows_in = picked[e]
        for c in range(0, inner.shape[1], 256):
            gate = jnp.dot(rows_in, wg[e, :, c : c + 256], preferred_element_type=F32)
            up = jnp.dot(rows_in, wu[e, :, c : c + 256], preferred_element_type=F32)
            inner[:, c : c + 256] = (gate / (1.0 + jnp.exp(-gate)) * up).astype(BF16)
        scale = jnp.concatenate(
            [
                jnp.sum(
                    jnp.where(
                        pair_hits(e, b),
                        gate_row[pl.ds(e, 1), b * span : (b + 1) * span],
                        0.0,
                    ),
                    axis=1,
                    keepdims=True,
                )
                for b in range(pairs)
            ],
            axis=0,
        )
        for c in range(0, width, chunk):
            answer = jnp.dot(inner[...], wd[e, :, c : c + chunk], preferred_element_type=F32)
            answer = (answer * scale).astype(BF16)
            for b in range(pairs):
                first = pl.multiple_of(e * slots, slots)
                answered[b, pl.ds(first, slots), c : c + chunk] = answer[
                    b * slots : (b + 1) * slots
                ]

    lane = lax.broadcasted_iota(jnp.int32, (span, slots), 1)
    for b in range(pairs):
        there = slice(b * span, (b + 1) * span)
        spreader = jnp.concatenate(
            [
                jnp.where(lane == slot_col[there, e : e + 1], 1.0, 0.0).astype(BF16)
                for e in range(exp_local)
            ],
            axis=1,
        )
        for c in range(0, width, chunk):
            sums = jnp.dot(
                spreader, answered[b, :, c : c + chunk], preferred_element_type=F32
            ).astype(BF16)
            for side in range(2):
                out, at = targets[2 * b + side]
                out[at * rows : (at + 1) * rows, c : c + chunk] = sums[
                    side * rows : (side + 1) * rows
                ]


def experts(blocks, layout, route, w_gate, w_up, w_down):
    count = len(blocks)
    pieces, spec = flatten(blocks)
    parts = sum(len(one) for one in spec)
    rows, width = blocks[0][0][2], pieces[0].shape[1]
    exp_local, _, hidden = w_gate.shape
    pairs = count // 2
    slots = 2 * CAP
    work = exp_local * pairs * slots
    return pl.pallas_call(
        functools.partial(expert_kernel, spec, rows, layout),
        out_shape=tuple(
            jax.ShapeDtypeStruct((many * rows, width), BF16)
            for many in layout
        ),
        in_specs=[vmem()] * 3 + [ANY] * (len(pieces) + 3),
        out_specs=(vmem(),) * len(layout),
        scratch_shapes=[
            pltpu.VMEM((count * rows, width), BF16),
            pltpu.VMEM(w_gate.shape, BF16),
            pltpu.VMEM(w_up.shape, BF16),
            pltpu.VMEM(w_down.shape, BF16),
            pltpu.VMEM((exp_local, pairs * slots, width), BF16),
            pltpu.VMEM((pairs, exp_local * slots, width), BF16),
            pltpu.VMEM((pairs * slots, hidden), BF16),
            pltpu.SemaphoreType.DMA((parts,)),
            pltpu.SemaphoreType.DMA((exp_local, 3)),
        ],
        compiler_params=params(),
        cost_estimate=pl.CostEstimate(
            flops=2 * work * width * (3 * hidden + 4 * rows),
            bytes_accessed=2 * (3 * w_gate.size + 2 * count * rows * width),
            transcendentals=work * hidden,
        ),
        name="experts",
    )(*route, *pieces, w_gate, w_up, w_down)


def packed_routes(routes, route_gates, lanes):
    parts = [routes.T.astype(BF16)]
    rest = route_gates.T
    for _ in range(3):
        term = lax.reduce_precision(rest, 8, 7)
        parts.append(term.astype(BF16))
        rest = rest - term
    per = len(parts) * LANES // lanes
    return jnp.concatenate(
        [jnp.concatenate(parts[i : i + per], axis=0) for i in range(0, len(parts), per)], axis=1
    )


def route_kernel(spec, first_expert, *refs):
    count = len(spec)
    sources = refs[:-5]
    slot_row, gate_row, slot_col, packed, sems = refs[-5:]
    exp_local = slot_row.shape[0]
    tall = packed.shape[1]
    copies = [
        pltpu.make_async_copy(
            sources[array].at[pl.ds(there + rows - tall, tall), pl.ds(0, packed.shape[2])],
            packed.at[k],
            sems.at[k],
        )
        for k, (array, there, rows) in enumerate(pieces[-1] for pieces in spec)
    ]
    for copy in copies:
        copy.start()
    for copy in copies:
        copy.wait()
    here = lax.broadcasted_iota(jnp.int32, (LANES, LANES), 1)
    there = lax.broadcasted_iota(jnp.int32, (LANES, LANES), 0)
    earlier = jnp.where(there < here, 1.0, 0.0).astype(BF16)
    choices = tall * packed.shape[2] // (4 * LANES)
    for k in range(count):
        block = packed[k].astype(F32)
        parts = [
            block[r : r + choices, c : c + LANES]
            for c in range(0, packed.shape[2], LANES)
            for r in range(0, tall, choices)
        ]
        named = parts[0]
        gates = parts[1] + parts[2] + parts[3]
        hits, shares = [], []
        for e in range(exp_local):
            match = named == (first_expert[0] + e).astype(F32)
            hits.append(jnp.max(jnp.where(match, 1.0, 0.0), axis=0, keepdims=True))
            shares.append(jnp.sum(jnp.where(match, gates, 0.0), axis=0, keepdims=True))
        hits += [jnp.zeros((1, LANES), F32)] * (8 - exp_local)
        hit = jnp.concatenate(hits, axis=0)
        rank = jnp.dot(hit.astype(BF16), earlier, preferred_element_type=F32)
        slot = jnp.where(hit > 0.0, rank + float(k % 2 * CAP), -1.0)
        lanes = slice(k * LANES, (k + 1) * LANES)
        slot_row[:, lanes] = slot[:exp_local].astype(jnp.int32)
        gate_row[:, lanes] = jnp.concatenate(shares, axis=0)
        slot_col[lanes, :] = slot.T.astype(jnp.int32)


def route_tables(sources, tall, lanes, first_expert, exp_local):
    count = len(sources)
    sources, spec = flatten(sources)
    tokens = count * LANES
    return pl.pallas_call(
        functools.partial(route_kernel, spec),
        out_shape=(
            jax.ShapeDtypeStruct((exp_local, tokens), jnp.int32),
            jax.ShapeDtypeStruct((exp_local, tokens), F32),
            jax.ShapeDtypeStruct((tokens, 8), jnp.int32),
        ),
        in_specs=[SMEM] + [ANY] * len(sources),
        out_specs=(vmem(), vmem(), vmem()),
        scratch_shapes=[
            pltpu.VMEM((count, tall, lanes), BF16),
            pltpu.SemaphoreType.DMA((count,)),
        ],
        compiler_params=params(),
        cost_estimate=pl.CostEstimate(
            flops=3 * 10**9, bytes_accessed=10**6, transcendentals=0
        ),
        name="route_tables",
    )(first_expert, *sources)


def local(
    tokens,
    segments,
    group_ids,
    prefix_owner,
    slab_fill,
    prefix_cache,
    attn_gain,
    w_query,
    w_keyval,
    w_out,
    ffn_gain,
    routes,
    route_gates,
    w_gate,
    w_up,
    w_down,
):
    tok_count = lax.axis_size("tok")
    groups = lax.axis_size("head")
    me_tok = lax.axis_index("tok")
    me_head = lax.axis_index("head")
    rows_dev, width = tokens.shape
    row_len = rows_dev * groups
    row_first = me_tok * row_len
    kv_local = w_keyval.shape[1] // (2 * HS)
    q_local = w_query.shape[1] // HS
    origins = plane_origins()

    half = rows_dev // 2
    turns = [(tokens[:half], tokens[half:])]

    def turn_on(tie):
        turns.append(tuple(next_turn(after(part, tie), "head") for part in turns[-1]))

    for _ in range(groups // 2):
        turn_on(None)

    steps = jnp.arange(groups, dtype=jnp.int32)
    block_of = (me_head - steps) % groups
    token_id = row_first + block_of[:, None] * rows_dev + jnp.arange(rows_dev, dtype=jnp.int32)
    row_segs = lax.dynamic_slice_in_dim(segments, row_first, row_len, 0).reshape(groups, rows_dev)
    segs = jnp.sum(
        jnp.where((block_of[:, None] == steps[None, :])[:, :, None], row_segs[None], 0), axis=1
    )
    requests = jnp.arange(group_ids.shape[0], dtype=jnp.int32)
    starts = jnp.sum((segments[None, :] < requests[:, None]).astype(jnp.int32), axis=1)
    begin = lookup(starts, segs)
    slab = lookup(lookup(prefix_owner, group_ids), segs)
    fill = lookup(slab_fill, slab)
    position = fill + token_id - begin
    steps_idx = jnp.arange(HS // 2, dtype=F32)
    inverse = jnp.exp(steps_idx * (-2.0 * jnp.log(10000.0) / HS))
    angles = position.astype(F32)[:, :, None] * inverse
    cosine = jnp.cos(angles)
    sine = jnp.sin(angles)
    cos = jnp.concatenate([cosine] * 4, axis=2)
    sin = jnp.concatenate([-sine, sine, -sine, sine], axis=2)
    info = jnp.stack([slab, begin, token_id, token_id], axis=2)
    place = token_id[:, 0]
    backs = jnp.arange(groups + 1, dtype=jnp.int32)
    read = jnp.any(slab[:, :, None] == origins, axis=1).astype(jnp.int32)
    spot = jnp.arange(read.shape[1], dtype=jnp.int32)
    rank = jnp.sum(jnp.where(spot[:, None] < spot[None, :], read[:, :, None], 0), axis=1)
    tables = {
        "near_list": (steps[:, None] + backs[None, :]) % groups
        + jnp.where(block_of[:, None] >= backs[None, :], groups, 0),
        "reach": (begin[:, 0] < place - rows_dev).astype(jnp.int32),
        "read": read,
        "slab_list": jnp.sum(
            jnp.where(
                (rank[:, :, None] == spot[None, None, :]) & (read[:, :, None] != 0),
                spot[None, :, None],
                0,
            ),
            axis=1,
        ),
        "slab_count": jnp.sum(read, axis=1),
        "fill": lookup(slab_fill, origins),
        "slab_id": origins,
        "place": jnp.concatenate([place - row_len, place]),
    }

    missing = -w_query.shape[1] % LANES
    if missing:
        w_query = jnp.pad(w_query, ((0, 0), (0, missing)))
    lanes = prefix_cache.shape[1]
    packed = packed_routes(routes, route_gates, lanes)
    prefix_rows = after(jnp.concatenate([prefix_cache, packed], axis=0), turns[1][0])
    neighbours = to_neighbours(prefix_rows)

    queries, own, prev = [], [], []
    for some in (slice(0, groups // 2), slice(groups // 2, groups)):
        while len(turns) < some.stop:
            turn_on((own[0], tables, info, neighbours))
        pieces = [piece for parts in turns[some] for piece in parts]
        query, keyval = project(
            after(pieces, prev[0]) if prev else pieces,
            attn_gain[None, :],
            w_query,
            w_keyval,
            cos[some],
            sin[some],
            kv_local,
            q_local,
        )
        queries += query
        own.append(keyval)
        prev.append(lax.ppermute(keyval, "tok", [(i, i + 1) for i in range(tok_count - 1)]))

    def exchanged(block, j):
        return lax.ppermute(block, "head", [(i, (i - j) % groups) for i in range(groups)])

    cached = to_plane(prefix_rows, neighbours, own[1])

    near = prev + own

    def term(j, held_as):
        return attend(j, tables, info, queries[j], near, cached, w_out, q_local, held_as)

    down = groups // 2
    up = groups - 1 - down
    lower = upper = None
    for turn in range(down):
        here = term(down - turn, BF16)
        if lower is not None:
            here = (here.astype(F32) + lower.astype(F32)).astype(BF16)
        lower = exchanged(here, 1)
        if turn < up:
            here = term(groups - up + turn, BF16)
            if upper is not None:
                here = (here.astype(F32) + upper.astype(F32)).astype(BF16)
            upper = exchanged(here, groups - 1)
    terms = [lower] if upper is None else [lower, upper]
    own_term = term(0, F32)
    exp_local = w_gate.shape[0]
    route = route_tables(
        cached,
        packed.shape[0],
        lanes,
        (me_tok * exp_local).astype(jnp.int32).reshape(1),
        exp_local,
    )
    hidden, expert_in = add_and_norm(tokens, ffn_gain[None, :], own_term, after(terms, route))

    def chosen(blocks, layout):
        return experts(blocks, layout, route, w_gate, w_up, w_down)

    if tok_count != 8:
        every = lax.all_gather(expert_in, "tok", axis=0, tiled=True)
        blocks = [[(every, k * rows_dev, rows_dev)] for k in range(tok_count)]
        (sums,) = chosen(blocks, (tok_count,))
        summed = lax.psum_scatter(sums, "tok", scatter_dimension=0, tiled=True).astype(F32)
        return (hidden + summed).astype(BF16)

    first, second, partner = cube_routes()

    def to_partner(array):
        return lax.ppermute(array, "tok", partner)

    one = lax.ppermute(expert_in, "tok", first)
    two = lax.ppermute(expert_in, "tok", second)
    three = [
        lax.ppermute(one[:half], "tok", second),
        lax.ppermute(two[half:], "tok", first),
    ]
    mine = [[expert_in], [one], [two], three]
    blocks = [
        [(piece, 0, piece.shape[0]) for piece in pieces]
        for pieces in mine + [[to_partner(piece) for piece in pieces] for pieces in mine]
    ]
    near, far, last = chosen(blocks, (4, 3, 1))
    return (hidden + plane_sum(near, far, last, rows_dev)).astype(BF16)


def solution(mesh):
    return jax.shard_map(
        local,
        mesh=mesh,
        in_specs=(
            P(("tok", "head"), None),
            P(),
            P(),
            P(),
            P(),
            P("tok", "head"),
            P(),
            P(None, "head"),
            P(None, "head"),
            P("head", None),
            P(),
            P(("tok", "head"), None),
            P(("tok", "head"), None),
            P("tok", None, None),
            P("tok", None, None),
            P("tok", None, None),
        ),
        out_specs=P(("tok", "head"), None),
        check_vma=False,
    )
```

```python
import functools

import jax
import jax.numpy as jnp
from jax import lax
from jax.experimental import pallas as pl
from jax.experimental.pallas import tpu as pltpu
from jax.sharding import PartitionSpec as P

HS = 64
CAP = 64
PREFIX = 512
LANES = 128
NEG_FILL = -1e30
NORM_EPS = 1e-06
F32 = jnp.float32
BF16 = jnp.bfloat16
VMEM_BYTES = 56 * 1024 * 1024


def vmem(*shape):
    return pl.BlockSpec(memory_space=pltpu.VMEM)


ANY = pl.BlockSpec(memory_space=pl.ANY)
SMEM = pl.BlockSpec(memory_space=pltpu.SMEM)


def params(**more):
    return pltpu.CompilerParams(vmem_limit_bytes=VMEM_BYTES, **more)


def next_turn(block, axis):
    count = lax.axis_size(axis)
    return lax.ppermute(block, axis, [(i, (i + 1) % count) for i in range(count)])


def cube_routes():
    first = [(t, t ^ (2 if t & 1 else 4)) for t in range(8)]
    second = [(t, t ^ (4 if t & 1 else 2)) for t in range(8)]
    partner = [(t, t ^ 1) for t in range(8)]
    return first, second, partner


def plane_origins():
    count = lax.axis_size("tok")
    if count != 8:
        return jnp.arange(count, dtype=jnp.int32)
    me = lax.axis_index("tok")
    one = jnp.where(me % 2 == 0, 4, 2)
    two = 6 - one
    other = me ^ 1
    return jnp.stack(
        [me, me ^ one, me ^ two, me ^ 6, other, other ^ two, other ^ one, other ^ 6]
    ).astype(jnp.int32)


def to_neighbours(block):
    if lax.axis_size("tok") != 8:
        return []
    first, second, _ = cube_routes()
    return [lax.ppermute(block, "tok", first), lax.ppermute(block, "tok", second)]


def to_plane(block, neighbours, tie):
    count = lax.axis_size("tok")
    rows = block.shape[0]
    if count != 8:
        whole = lax.all_gather(block, "tok", axis=0, tiled=True)
        return [[(whole, i * rows, rows)] for i in range(count)]
    _, second, partner = cube_routes()
    across = lax.ppermute(neighbours[0], "tok", second)
    every = jnp.concatenate(after([block, *neighbours, across], tie), axis=0)
    return [
        [(side, i * rows, rows)]
        for side in (every, lax.ppermute(every, "tok", partner))
        for i in range(4)
    ]


def flatten(blocks):
    arrays, spec = [], []
    for pieces in blocks:
        here = []
        for array, first, rows in pieces:
            known = [i for i, other in enumerate(arrays) if other is array]
            if not known:
                known = [len(arrays)]
                arrays.append(array)
            here.append((known[0], first, rows))
        spec.append(here)
    return arrays, spec


def row_ranges(pieces, first, count):
    base = 0
    for array, start, rows in pieces:
        low, high = max(first, base), min(first + count, base + rows)
        if low < high:
            yield array, start + low - base, low - first, high - low
        base += rows


def after(value, tie):
    return value if tie is None else lax.optimization_barrier((value, tie))[0]


def plane_sum(near, far, last, rows):
    first, second, partner = cube_routes()
    half = rows // 2
    got_last = lax.ppermute(last, "tok", partner)
    got = lax.ppermute(far, "tok", partner)
    three = (near[3 * rows :].astype(F32) + got_last.astype(F32)).astype(BF16)
    across_upper = lax.ppermute(three[:half], "tok", second)
    across_lower = lax.ppermute(three[half:], "tok", first)
    near, got = after((near, got), (across_upper, across_lower))

    def pair(block):
        here = slice(block * rows, (block + 1) * rows)
        return near[here].astype(F32) + got[here].astype(F32)

    nothing = jnp.zeros(across_upper.shape, F32)
    add_upper = jnp.concatenate([across_upper.astype(F32), nothing], axis=0)
    add_lower = jnp.concatenate([nothing, across_lower.astype(F32)], axis=0)
    along = lax.ppermute((pair(1) + add_upper).astype(BF16), "tok", first)
    beside = lax.ppermute((pair(2) + add_lower).astype(BF16), "tok", second)
    return pair(0) + beside.astype(F32) + along.astype(F32)


BEGIN, PLACE, BLOCK = 120, 121, 122


def table_kernel(groups, me, owner_of, fill_of, group_ids, inverse, segs, *outs):
    cosines, sines, info, marks = outs[:2], outs[2:4], outs[4], outs[5]
    ids = group_ids[...]
    owner = jnp.zeros(ids.shape, F32)
    fill = jnp.zeros(ids.shape, F32)
    for g in range(owner_of.shape[0]):
        owner = jnp.where(ids == g, owner_of[g].astype(F32), owner)
        fill = jnp.where(ids == g, fill_of[owner_of[g]].astype(F32), fill)
    square = (LANES, LANES)
    row = lax.broadcasted_iota(jnp.int32, square, 0)
    lane = lax.broadcasted_iota(jnp.int32, square, 1)
    request = lax.broadcasted_iota(jnp.int32, (LANES, ids.shape[1]), 1).astype(F32)
    sign = jnp.where(lane % HS < HS // 2, -1.0, 1.0)
    many = segs.shape[0]
    for j in range(groups):
        block = lax.rem(me[1] - j + groups, groups)
        which = me[0] * groups + block
        here = segs[pl.ds(which, 1), :].astype(F32)
        own = jnp.sum(jnp.where(row == lane, here, 0.0), axis=1, keepdims=True)
        wide = jnp.broadcast_to(own, square)
        earlier = jnp.zeros(square, F32)
        for u in range(many):
            earlier += jnp.where(segs[u : u + 1, :].astype(F32) < wide, 1.0, 0.0)
        begin = jnp.sum(earlier, axis=1, keepdims=True)
        match = own == request
        slab = jnp.sum(jnp.where(match, owner, 0.0), axis=1, keepdims=True)
        start = jnp.sum(jnp.where(match, fill, 0.0), axis=1, keepdims=True)
        first = which * LANES
        place = (first + row).astype(F32)
        angles = (start + place - begin) * inverse[...]
        side, at = (0, j) if j < groups // 2 else (1, j - groups // 2)
        cosines[side][at * LANES : (at + 1) * LANES, :] = jnp.cos(angles)
        sines[side][at * LANES : (at + 1) * LANES, :] = jnp.sin(angles) * sign
        slab_wide = jnp.broadcast_to(slab, square).astype(jnp.int32)
        begin_wide = jnp.broadcast_to(begin, square)
        info[j, 0] = slab_wide
        info[j, 1] = begin_wide.astype(jnp.int32)
        read = jnp.max(jnp.where(slab_wide == lane, 1.0, 0.0), axis=0, keepdims=True)
        lowest = jnp.min(begin_wide, axis=0, keepdims=True)
        spot = lane[:1]
        line = jnp.where(spot == BEGIN, lowest, read).astype(jnp.int32)
        line = jnp.where(spot == PLACE, first, line)
        marks[j : j + 1, :] = jnp.where(spot == BLOCK, block, line)


def row_tables(groups, me, prefix_owner, slab_fill, group_ids, inverse, segments):
    half = jax.ShapeDtypeStruct((groups // 2 * LANES, LANES), F32)
    outs = pl.pallas_call(
        functools.partial(table_kernel, groups),
        out_shape=(half,) * 4
        + (
            jax.ShapeDtypeStruct((groups, 2, LANES, LANES), jnp.int32),
            jax.ShapeDtypeStruct((groups, LANES), jnp.int32),
        ),
        in_specs=[SMEM] * 3 + [vmem()] * 3,
        out_specs=(vmem(),) * 6,
        compiler_params=params(),
        cost_estimate=pl.CostEstimate(
            flops=4 * 10**9, bytes_accessed=10**6, transcendentals=10**5
        ),
        name="row_tables",
    )(
        me,
        prefix_owner,
        slab_fill,
        group_ids.reshape(1, -1),
        inverse.reshape(1, LANES),
        segments.reshape(-1, LANES),
    )
    return outs[:2], outs[2:4], outs[4], outs[5]


def project_kernel(blocks, kv_local, q_local, *refs):
    pieces = refs[:blocks]
    gain, wq, wkv, cos, sin = refs[blocks : blocks + 5]
    q_outs = refs[blocks + 5 : 2 * blocks + 5]
    kv_out, normed = refs[2 * blocks + 5 :]
    half = pieces[0].shape[0]
    for i, piece in enumerate(pieces):
        wide = piece[...].astype(F32)
        spread = jnp.mean(wide * wide, axis=-1, keepdims=True)
        normed[i * half : (i + 1) * half, :] = (
            wide * lax.rsqrt(spread + NORM_EPS) * gain[...]
        ).astype(BF16)
    share = q_local // kv_local
    rows = normed.shape[0]
    rows_dev = rows // blocks
    lane = lax.broadcasted_iota(jnp.int32, (rows, LANES), 1)
    low_half = lane % HS < HS // 2
    low_head = lane < HS

    def turned(values, cosine, sine):
        swapped = jnp.where(
            low_half, pltpu.roll(values, LANES - HS // 2, 1), pltpu.roll(values, HS // 2, 1)
        )
        return values * cosine + swapped * sine

    cosine = cos[...]
    sine = sin[...]
    keyval = jnp.dot(normed[...], wkv[...], preferred_element_type=F32)
    cosine_kv = jnp.where(low_head, cosine, 1.0)
    sine_kv = jnp.where(low_head, sine, 0.0)
    for g in range(kv_local):
        here = slice(g * LANES, (g + 1) * LANES)
        kv_out[:, here] = turned(keyval[:, here], cosine_kv, sine_kv).astype(BF16)
    queries = jnp.dot(normed[...], wq[...], preferred_element_type=F32)
    for pair in range(queries.shape[1] // LANES):
        both = turned(queries[:, pair * LANES : (pair + 1) * LANES], cosine, sine) * HS ** (-0.5)
        for odd in range(2):
            head = 2 * pair + odd
            if head >= q_local:
                continue
            alone = pltpu.roll(both, HS, 1) if odd else both
            alone = jnp.where(low_head, alone, 0.0).astype(BF16)
            group, slot = head // share, head % share
            for j in range(blocks):
                q_outs[j][group, slot * rows_dev : (slot + 1) * rows_dev, :] = alone[
                    j * rows_dev : (j + 1) * rows_dev
                ]


def project(pieces, gain, w_query, w_keyval, cos, sin, kv_local, q_local):
    blocks = len(pieces)
    rows_dev, width = pieces[0].shape
    share = q_local // kv_local
    outs = pl.pallas_call(
        functools.partial(project_kernel, blocks, kv_local, q_local),
        out_shape=[jax.ShapeDtypeStruct((kv_local, share * rows_dev, LANES), BF16)] * blocks
        + [jax.ShapeDtypeStruct((blocks * rows_dev, kv_local * LANES), BF16)],
        in_specs=[vmem()] * (blocks + 5),
        out_specs=[vmem()] * (blocks + 1),
        scratch_shapes=[pltpu.VMEM((blocks * rows_dev, width), BF16)],
        compiler_params=params(),
        cost_estimate=pl.CostEstimate(
            flops=4 * 10**9, bytes_accessed=4 * 10**6, transcendentals=blocks * rows_dev
        ),
        name="norm_project_rotate",
    )(*pieces, gain, w_query, w_keyval, cos, sin)
    return list(outs[:-1]), outs[-1]


def attend_kernel(block, near_parts, slab_spec, q_local, *refs):
    marks, slab_id, fill_of, query, info = refs[:5]
    near_refs = refs[5 : 5 + near_parts]
    slab_refs = refs[5 + near_parts : -18]
    w_ref, out = refs[-18:-16]
    near, far, scores, peak, total, accum, begin, owner, heads, mixed, w_all, held = refs[-16:-4]
    near_sems, slab_sems, w_sem, info_sem = refs[-4:]
    parts = info.shape[0]
    kv_local, stack, _ = query.shape
    rows_dev = info.shape[2]
    share = stack // rows_dev
    cuts = PREFIX // LANES
    window = parts + 1
    wide = (stack, LANES)
    lane = lax.broadcasted_iota(jnp.int32, (1, LANES), 1)

    def lanes(ref, g, rows, start=0):
        return ref.at[pl.ds(start, rows), pl.ds(g * LANES, LANES)]

    copies = []
    base = 0
    for i, ref in enumerate(near_refs):
        for g in range(kv_local):
            copies.append(
                pltpu.make_async_copy(
                    lanes(ref, g, ref.shape[0]),
                    near.at[g, pl.ds(base, ref.shape[0])],
                    near_sems.at[i, g],
                )
            )
        base += ref.shape[0]

    def each_slab(act):
        for i, [(array, start, _)] in enumerate(slab_spec):
            @pl.when(marks[block, slab_id[i]] != 0)
            def _(i=i, array=array, start=start):
                for g in range(kv_local):
                    act(
                        pltpu.make_async_copy(
                            lanes(slab_refs[array], g, PREFIX, start),
                            far.at[g, pl.ds(i * PREFIX, PREFIX)],
                            slab_sems.at[i, g],
                        )
                    )

    w_copy = pltpu.make_async_copy(w_ref, w_all, w_sem)
    info_copy = pltpu.make_async_copy(info.at[block], held, info_sem)
    info_copy.start()
    for copy in copies:
        copy.start()
    each_slab(lambda copy: copy.start())
    w_copy.start()
    info_copy.wait()
    for ref, kind in ((owner, 0), (begin, 1)):
        ref[...] = jnp.concatenate([held[kind]] * share, axis=0)
    row = lax.broadcasted_iota(jnp.int32, wide, 0)
    order = row - lax.div(row, rows_dev) * rows_dev
    for copy in copies:
        copy.wait()

    def rows_near(g, back):
        unit = lax.rem(block + back, parts) + jnp.where(marks[block, BLOCK] >= back, parts, 0)
        return near[g, pl.ds(pl.multiple_of(unit * rows_dev, rows_dev), rows_dev), :]

    def rows_window(g, backs):
        return jnp.concatenate([rows_near(g, back) for back in backs], axis=0)

    def rows_far(g, slab):
        return far[g, pl.ds(pl.multiple_of(slab * PREFIX, PREFIX), PREFIX), :]

    def score(g, rows):
        return lax.dot_general(
            query[g], rows, (((1,), (1,)), ((), ())), preferred_element_type=F32
        )

    def near_scores(backs, opening):
        for g in range(kv_local):
            every = score(g, rows_window(g, backs))
            top = None if opening else peak[g]
            for at, back in enumerate(backs):
                there = marks[block, PLACE] - back * rows_dev + lane
                seen = there >= begin[...]
                if back == 0:
                    seen = seen & (lane <= order)
                here = every[:, at * LANES : (at + 1) * LANES]
                here = jnp.where(seen, here, NEG_FILL)
                scores[g, back] = here
                top = here if top is None else jnp.maximum(top, here)
            peak[g] = top

    def far_scores(slab):
        mine = owner[...] == slab_id[slab]
        for g in range(kv_local):
            every = score(g, rows_far(g, slab))
            top = None
            for c in range(cuts):
                here = every[:, c * LANES : (c + 1) * LANES]
                if (c + 1) * LANES > PREFIX // 2:
                    here = jnp.where(lane + c * LANES < fill_of[slab_id[slab]], here, NEG_FILL)
                scores[g, window + slab * cuts + c] = here
                top = here if top is None else jnp.maximum(top, here)
            old = peak[g]
            peak[g] = jnp.where(mine, jnp.maximum(old, top), old)

    def near_values(backs, opening):
        for g in range(kv_local):
            weights = [jnp.exp(scores[g, back] - peak[g]) for back in backs]
            packed = jnp.concatenate([part.astype(BF16) for part in weights], axis=1)
            summed = functools.reduce(jnp.add, weights)
            product = jnp.dot(packed, rows_window(g, backs), preferred_element_type=F32)
            if opening:
                total[g] = summed
                accum[g] = product
            else:
                total[g] += summed
                accum[g] += product

    def far_values(slab):
        mine = owner[...] == slab_id[slab]
        for g in range(kv_local):
            shift = jnp.where(mine, peak[g], -NEG_FILL)
            weights = [
                jnp.exp(scores[g, window + slab * cuts + c] - shift) for c in range(cuts)
            ]
            packed = jnp.concatenate([part.astype(BF16) for part in weights], axis=1)
            total[g] += functools.reduce(jnp.add, weights)
            accum[g] += jnp.dot(packed, rows_far(g, slab), preferred_element_type=F32)

    def sweep(near_body, far_body, between=None):
        near_body((0, 1), True)

        @pl.when(marks[block, BEGIN] < marks[block, PLACE] - rows_dev)
        def _():
            near_body(tuple(range(2, window)), False)

        if between is not None:
            between()

        @pl.loop(0, len(slab_spec))
        def _(slab):
            @pl.when(marks[block, slab_id[slab]] != 0)
            def _():
                far_body(slab)

    sweep(near_scores, far_scores, lambda: each_slab(lambda copy: copy.wait()))
    for g in range(kv_local):
        peak[g] = jnp.broadcast_to(jnp.max(peak[g], axis=1, keepdims=True), wide)
    sweep(near_values, far_values)
    for g in range(kv_local):
        result = accum[g] / jnp.sum(total[g], axis=1, keepdims=True)
        for slot in range(share):
            heads[g * share + slot] = result[slot * rows_dev : (slot + 1) * rows_dev]

    low = lax.broadcasted_iota(jnp.int32, (rows_dev, LANES), 1) < HS
    for pair in range((q_local + 1) // 2):
        left = pltpu.roll(heads[2 * pair], HS, 1)
        here = slice(pair * LANES, (pair + 1) * LANES)
        if 2 * pair + 1 < q_local:
            mixed[:, here] = jnp.where(low, left, heads[2 * pair + 1]).astype(BF16)
        else:
            mixed[:, pair * LANES :] = left[:, :HS].astype(BF16)
    w_copy.wait()
    out[...] = jnp.dot(mixed[...], w_all[...], preferred_element_type=F32).astype(out.dtype)


def attend(block, marks, origins, slab_fill, info, query, near, slabs, w_out, q_local, held_as):
    parts = info.shape[0]
    kv_local, stack, _ = query.shape
    rows_dev = info.shape[2]
    units = parts + 1 + len(slabs) * (PREFIX // LANES)
    wide = (stack, LANES)
    arrays, slab_spec = flatten(slabs)
    return pl.pallas_call(
        functools.partial(attend_kernel, block, len(near), slab_spec, q_local),
        out_shape=jax.ShapeDtypeStruct((rows_dev, w_out.shape[1]), held_as),
        in_specs=[SMEM] * 3 + [vmem()] + [ANY] * (len(near) + len(arrays) + 2),
        out_specs=vmem(),
        scratch_shapes=[
            pltpu.VMEM((kv_local, 2 * parts * rows_dev, LANES), BF16),
            pltpu.VMEM((kv_local, len(slabs) * PREFIX, LANES), BF16),
            pltpu.VMEM((kv_local, units) + wide, F32),
            pltpu.VMEM((kv_local,) + wide, F32),
            pltpu.VMEM((kv_local,) + wide, F32),
            pltpu.VMEM((kv_local,) + wide, F32),
            pltpu.VMEM(wide, jnp.int32),
            pltpu.VMEM(wide, jnp.int32),
            pltpu.VMEM((q_local, rows_dev, LANES), F32),
            pltpu.VMEM((rows_dev, q_local * HS), BF16),
            pltpu.VMEM(w_out.shape, BF16),
            pltpu.VMEM(info.shape[1:], jnp.int32),
            pltpu.SemaphoreType.DMA((len(near), kv_local)),
            pltpu.SemaphoreType.DMA((len(slabs), kv_local)),
            pltpu.SemaphoreType.DMA,
            pltpu.SemaphoreType.DMA,
        ],
        compiler_params=params(),
        cost_estimate=pl.CostEstimate(
            flops=8 * 10**9, bytes_accessed=4 * 10**6, transcendentals=10**6
        ),
        name="attend",
    )(
        marks,
        origins,
        slab_fill,
        query,
        info,
        *near,
        *arrays,
        w_out,
    )


def hidden_kernel(tokens, gain, own, *refs):
    others = refs[:-2]
    hidden, expert_in = refs[-2:]
    total = tokens[...].astype(F32) + own[...]
    for other in others:
        total += other[...].astype(F32)
    hidden[...] = total
    spread = jnp.mean(total * total, axis=-1, keepdims=True)
    expert_in[...] = (total * lax.rsqrt(spread + NORM_EPS) * gain[...]).astype(BF16)


def add_and_norm(tokens, gain, own, others):
    return pl.pallas_call(
        hidden_kernel,
        out_shape=(
            jax.ShapeDtypeStruct(tokens.shape, F32),
            jax.ShapeDtypeStruct(tokens.shape, BF16),
        ),
        in_specs=[vmem()] * (3 + len(others)),
        out_specs=(vmem(), vmem()),
        compiler_params=params(),
        cost_estimate=pl.CostEstimate(
            flops=10**9, bytes_accessed=16 * tokens.size, transcendentals=tokens.shape[0]
        ),
        name="add_and_norm",
    )(tokens, gain, own, *others)


def expert_kernel(spec, rows, layout, slot_row, gate_row, slot_col, *refs):
    count = len(spec)
    x_refs = refs[: -12 - len(layout)]
    wg_ref, wu_ref, wd_ref = refs[-12 - len(layout) : -9 - len(layout)]
    outs = refs[-9 - len(layout) : -9]
    x_all, wg, wu, wd, picked, answered, inner, x_sem, w_sem = refs[-9:]
    targets = [(out, i) for out, many in zip(outs, layout) for i in range(many)]
    exp_local = wg.shape[0]
    width = x_all.shape[1]
    span = 2 * rows
    slots = 2 * CAP
    pairs = count // 2
    chunk = 512

    x_copies = []
    base = 0
    for array, there, many_rows in [piece for pieces in spec for piece in pieces]:
        x_copies.append(
            pltpu.make_async_copy(
                x_refs[array].at[pl.ds(there, many_rows)],
                x_all.at[pl.ds(base, many_rows)],
                x_sem.at[len(x_copies)],
            )
        )
        base += many_rows
    for copy in x_copies:
        copy.start()

    def w_copies(e):
        return [
            pltpu.make_async_copy(source.at[e], target.at[e], w_sem.at[e, i])
            for i, (source, target) in enumerate(((wg_ref, wg), (wu_ref, wu), (wd_ref, wd)))
        ]

    for e in range(exp_local):
        for copy in w_copies(e):
            copy.start()
    for copy in x_copies:
        copy.wait()

    slot_iota = lax.broadcasted_iota(jnp.int32, (slots, span), 0)

    def pair_hits(e, b):
        there = slice(b * span, (b + 1) * span)
        return slot_iota == slot_row[pl.ds(e, 1), there]

    for b in range(pairs):
        hits = [jnp.where(pair_hits(e, b), 1.0, 0.0).astype(BF16) for e in range(exp_local)]
        chooser = jnp.concatenate(hits, axis=0)
        for c in range(0, width, chunk):
            found = jnp.dot(
                chooser,
                x_all[b * span : (b + 1) * span, c : c + chunk],
                preferred_element_type=F32,
            ).astype(BF16)
            for e in range(exp_local):
                picked[e, b * slots : (b + 1) * slots, c : c + chunk] = found[
                    e * slots : (e + 1) * slots
                ]

    @pl.loop(0, exp_local)
    def _(e):
        for copy in w_copies(e):
            copy.wait()
        rows_in = picked[e]
        for c in range(0, inner.shape[1], 256):
            gate = jnp.dot(rows_in, wg[e, :, c : c + 256], preferred_element_type=F32)
            up = jnp.dot(rows_in, wu[e, :, c : c + 256], preferred_element_type=F32)
            inner[:, c : c + 256] = (gate / (1.0 + jnp.exp(-gate)) * up).astype(BF16)
        scale = jnp.concatenate(
            [
                jnp.sum(
                    jnp.where(
                        pair_hits(e, b),
                        gate_row[pl.ds(e, 1), b * span : (b + 1) * span],
                        0.0,
                    ),
                    axis=1,
                    keepdims=True,
                )
                for b in range(pairs)
            ],
            axis=0,
        )
        for c in range(0, width, chunk):
            answer = jnp.dot(inner[...], wd[e, :, c : c + chunk], preferred_element_type=F32)
            answer = (answer * scale).astype(BF16)
            for b in range(pairs):
                first = pl.multiple_of(e * slots, slots)
                answered[b, pl.ds(first, slots), c : c + chunk] = answer[
                    b * slots : (b + 1) * slots
                ]

    lane = lax.broadcasted_iota(jnp.int32, (span, slots), 1)
    for b in range(pairs):
        there = slice(b * span, (b + 1) * span)
        spreader = jnp.concatenate(
            [
                jnp.where(lane == slot_col[there, e : e + 1], 1.0, 0.0).astype(BF16)
                for e in range(exp_local)
            ],
            axis=1,
        )
        for c in range(0, width, chunk):
            sums = jnp.dot(
                spreader, answered[b, :, c : c + chunk], preferred_element_type=F32
            ).astype(BF16)
            for side in range(2):
                out, at = targets[2 * b + side]
                out[at * rows : (at + 1) * rows, c : c + chunk] = sums[
                    side * rows : (side + 1) * rows
                ]


def experts(blocks, layout, route, w_gate, w_up, w_down):
    count = len(blocks)
    pieces, spec = flatten(blocks)
    parts = sum(len(one) for one in spec)
    rows, width = blocks[0][0][2], pieces[0].shape[1]
    exp_local, _, hidden = w_gate.shape
    pairs = count // 2
    slots = 2 * CAP
    work = exp_local * pairs * slots
    return pl.pallas_call(
        functools.partial(expert_kernel, spec, rows, layout),
        out_shape=tuple(
            jax.ShapeDtypeStruct((many * rows, width), BF16)
            for many in layout
        ),
        in_specs=[vmem()] * 3 + [ANY] * (len(pieces) + 3),
        out_specs=(vmem(),) * len(layout),
        scratch_shapes=[
            pltpu.VMEM((count * rows, width), BF16),
            pltpu.VMEM(w_gate.shape, BF16),
            pltpu.VMEM(w_up.shape, BF16),
            pltpu.VMEM(w_down.shape, BF16),
            pltpu.VMEM((exp_local, pairs * slots, width), BF16),
            pltpu.VMEM((pairs, exp_local * slots, width), BF16),
            pltpu.VMEM((pairs * slots, hidden), BF16),
            pltpu.SemaphoreType.DMA((parts,)),
            pltpu.SemaphoreType.DMA((exp_local, 3)),
        ],
        compiler_params=params(),
        cost_estimate=pl.CostEstimate(
            flops=2 * work * width * (3 * hidden + 4 * rows),
            bytes_accessed=2 * (3 * w_gate.size + 2 * count * rows * width),
            transcendentals=work * hidden,
        ),
        name="experts",
    )(*route, *pieces, w_gate, w_up, w_down)


def packed_routes(routes, route_gates, lanes):
    parts = [routes.T.astype(BF16)]
    rest = route_gates.T
    for _ in range(3):
        term = lax.reduce_precision(rest, 8, 7)
        parts.append(term.astype(BF16))
        rest = rest - term
    per = len(parts) * LANES // lanes
    return jnp.concatenate(
        [jnp.concatenate(parts[i : i + per], axis=0) for i in range(0, len(parts), per)], axis=1
    )


def route_kernel(spec, first_expert, *refs):
    count = len(spec)
    sources = refs[:-5]
    slot_row, gate_row, slot_col, packed, sems = refs[-5:]
    exp_local = slot_row.shape[0]
    tall = packed.shape[1]
    copies = [
        pltpu.make_async_copy(
            sources[array].at[pl.ds(there + rows - tall, tall), pl.ds(0, packed.shape[2])],
            packed.at[k],
            sems.at[k],
        )
        for k, (array, there, rows) in enumerate(pieces[-1] for pieces in spec)
    ]
    for copy in copies:
        copy.start()
    for copy in copies:
        copy.wait()
    here = lax.broadcasted_iota(jnp.int32, (LANES, LANES), 1)
    there = lax.broadcasted_iota(jnp.int32, (LANES, LANES), 0)
    earlier = jnp.where(there < here, 1.0, 0.0).astype(BF16)
    choices = tall * packed.shape[2] // (4 * LANES)
    for k in range(count):
        block = packed[k].astype(F32)
        parts = [
            block[r : r + choices, c : c + LANES]
            for c in range(0, packed.shape[2], LANES)
            for r in range(0, tall, choices)
        ]
        named = parts[0]
        gates = parts[1] + parts[2] + parts[3]
        hits, shares = [], []
        for e in range(exp_local):
            match = named == (first_expert[0] + e).astype(F32)
            hits.append(jnp.max(jnp.where(match, 1.0, 0.0), axis=0, keepdims=True))
            shares.append(jnp.sum(jnp.where(match, gates, 0.0), axis=0, keepdims=True))
        hits += [jnp.zeros((1, LANES), F32)] * (8 - exp_local)
        hit = jnp.concatenate(hits, axis=0)
        rank = jnp.dot(hit.astype(BF16), earlier, preferred_element_type=F32)
        slot = jnp.where(hit > 0.0, rank + float(k % 2 * CAP), -1.0)
        lanes = slice(k * LANES, (k + 1) * LANES)
        slot_row[:, lanes] = slot[:exp_local].astype(jnp.int32)
        gate_row[:, lanes] = jnp.concatenate(shares, axis=0)
        slot_col[lanes, :] = slot.T.astype(jnp.int32)


def route_tables(sources, tall, lanes, first_expert, exp_local):
    count = len(sources)
    sources, spec = flatten(sources)
    tokens = count * LANES
    return pl.pallas_call(
        functools.partial(route_kernel, spec),
        out_shape=(
            jax.ShapeDtypeStruct((exp_local, tokens), jnp.int32),
            jax.ShapeDtypeStruct((exp_local, tokens), F32),
            jax.ShapeDtypeStruct((tokens, 8), jnp.int32),
        ),
        in_specs=[SMEM] + [ANY] * len(sources),
        out_specs=(vmem(), vmem(), vmem()),
        scratch_shapes=[
            pltpu.VMEM((count, tall, lanes), BF16),
            pltpu.SemaphoreType.DMA((count,)),
        ],
        compiler_params=params(),
        cost_estimate=pl.CostEstimate(
            flops=3 * 10**9, bytes_accessed=10**6, transcendentals=0
        ),
        name="route_tables",
    )(first_expert, *sources)


def local(
    tokens,
    segments,
    group_ids,
    prefix_owner,
    slab_fill,
    prefix_cache,
    attn_gain,
    w_query,
    w_keyval,
    w_out,
    ffn_gain,
    routes,
    route_gates,
    w_gate,
    w_up,
    w_down,
):
    tok_count = lax.axis_size("tok")
    groups = lax.axis_size("head")
    me_tok = lax.axis_index("tok")
    me_head = lax.axis_index("head")
    rows_dev, width = tokens.shape
    kv_local = w_keyval.shape[1] // (2 * HS)
    q_local = w_query.shape[1] // HS
    origins = plane_origins()

    turns = [tokens]

    def turn_on(tie):
        turns.append(next_turn(after(turns[-1], tie), "head"))

    for _ in range(groups // 2):
        turn_on(None)

    steps_idx = jnp.arange(HS // 2, dtype=F32)
    inverse = jnp.exp(steps_idx * (-2.0 * jnp.log(10000.0) / HS))
    cos, sin, info, marks = row_tables(
        groups,
        jnp.stack([me_tok, me_head]).astype(jnp.int32),
        prefix_owner,
        slab_fill,
        group_ids,
        jnp.concatenate([inverse] * 4),
        segments,
    )

    missing = -w_query.shape[1] % LANES
    if missing:
        w_query = jnp.pad(w_query, ((0, 0), (0, missing)))

    lanes = prefix_cache.shape[1]
    packed = packed_routes(routes, route_gates, lanes)
    prefix_rows = after(jnp.concatenate([prefix_cache, packed], axis=0), turns[1])
    neighbours = to_neighbours(prefix_rows)

    queries, own, prev = [], [], []
    for some in (slice(0, groups // 2), slice(groups // 2, groups)):
        while len(turns) < some.stop:
            turn_on((own[0], neighbours))
        pieces = turns[some]
        query, keyval = project(
            after(pieces, prev[0]) if prev else pieces,
            attn_gain[None, :],
            w_query,
            w_keyval,
            cos[len(own)],
            sin[len(own)],
            kv_local,
            q_local,
        )
        queries += query
        own.append(keyval)
        prev.append(lax.ppermute(keyval, "tok", [(i, i + 1) for i in range(tok_count - 1)]))

    def exchanged(block, j):
        return lax.ppermute(block, "head", [(i, (i - j) % groups) for i in range(groups)])

    cached = to_plane(prefix_rows, neighbours, own[1])

    near = prev + own

    def term(j, held_as):
        return attend(
            j, marks, origins, slab_fill, info, queries[j], near, cached, w_out, q_local, held_as
        )

    down = groups // 2
    up = groups - 1 - down
    lower = upper = None
    for turn in range(down):
        here = term(down - turn, BF16)
        if lower is not None:
            here = (here.astype(F32) + lower.astype(F32)).astype(BF16)
        lower = exchanged(here, 1)
        if turn < up:
            here = term(groups - up + turn, BF16)
            if upper is not None:
                here = (here.astype(F32) + upper.astype(F32)).astype(BF16)
            upper = exchanged(here, groups - 1)
    terms = [lower] if upper is None else [lower, upper]
    own_term = term(0, F32)
    exp_local = w_gate.shape[0]
    route = route_tables(
        cached,
        packed.shape[0],
        lanes,
        (me_tok * exp_local).astype(jnp.int32).reshape(1),
        exp_local,
    )
    hidden, expert_in = add_and_norm(tokens, ffn_gain[None, :], own_term, after(terms, route))

    def chosen(blocks, layout):
        return experts(blocks, layout, route, w_gate, w_up, w_down)

    if tok_count != 8:
        every = lax.all_gather(expert_in, "tok", axis=0, tiled=True)
        blocks = [[(every, k * rows_dev, rows_dev)] for k in range(tok_count)]
        (sums,) = chosen(blocks, (tok_count,))
        summed = lax.psum_scatter(sums, "tok", scatter_dimension=0, tiled=True).astype(F32)
        return (hidden + summed).astype(BF16)

    first, second, partner = cube_routes()

    def to_partner(array):
        return lax.ppermute(array, "tok", partner)

    one = lax.ppermute(expert_in, "tok", first)
    two = lax.ppermute(expert_in, "tok", second)
    half = rows_dev // 2
    three = [
        lax.ppermute(one[:half], "tok", second),
        lax.ppermute(two[half:], "tok", first),
    ]
    mine = [[expert_in], [one], [two], three]
    blocks = [
        [(piece, 0, piece.shape[0]) for piece in pieces]
        for pieces in mine + [[to_partner(piece) for piece in pieces] for pieces in mine]
    ]
    near, far, last = chosen(blocks, (4, 3, 1))
    return (hidden + plane_sum(near, far, last, rows_dev)).astype(BF16)


def solution(mesh):
    return jax.shard_map(
        local,
        mesh=mesh,
        in_specs=(
            P(("tok", "head"), None),
            P(),
            P(),
            P(),
            P(),
            P("tok", "head"),
            P(),
            P(None, "head"),
            P(None, "head"),
            P("head", None),
            P(),
            P(("tok", "head"), None),
            P(("tok", "head"), None),
            P("tok", None, None),
            P("tok", None, None),
            P("tok", None, None),
        ),
        out_specs=P(("tok", "head"), None),
        check_vma=False,
    )
```

```python
import functools

import jax
import jax.numpy as jnp
from jax import lax
from jax.experimental import pallas as pl
from jax.experimental.pallas import tpu as pltpu
from jax.sharding import PartitionSpec as P

HS = 64
CAP = 64
PREFIX = 512
LANES = 128
NEG_FILL = -1e30
NORM_EPS = 1e-06
F32 = jnp.float32
BF16 = jnp.bfloat16
VMEM_BYTES = 56 * 1024 * 1024


def vmem(*shape):
    return pl.BlockSpec(memory_space=pltpu.VMEM)


ANY = pl.BlockSpec(memory_space=pl.ANY)
SMEM = pl.BlockSpec(memory_space=pltpu.SMEM)


def params(**more):
    return pltpu.CompilerParams(vmem_limit_bytes=VMEM_BYTES, **more)


def next_turn(block, axis):
    count = lax.axis_size(axis)
    return lax.ppermute(block, axis, [(i, (i + 1) % count) for i in range(count)])


def cube_routes():
    first = [(t, t ^ (2 if t & 1 else 4)) for t in range(8)]
    second = [(t, t ^ (4 if t & 1 else 2)) for t in range(8)]
    partner = [(t, t ^ 1) for t in range(8)]
    return first, second, partner


def plane_origins():
    count = lax.axis_size("tok")
    if count != 8:
        return jnp.arange(count, dtype=jnp.int32)
    me = lax.axis_index("tok")
    one = jnp.where(me % 2 == 0, 4, 2)
    two = 6 - one
    other = me ^ 1
    return jnp.stack(
        [me, me ^ one, me ^ two, me ^ 6, other, other ^ two, other ^ one, other ^ 6]
    ).astype(jnp.int32)


def to_neighbours(block):
    if lax.axis_size("tok") != 8:
        return []
    first, second, _ = cube_routes()
    return [lax.ppermute(block, "tok", first), lax.ppermute(block, "tok", second)]


def to_plane(block, neighbours, tie):
    count = lax.axis_size("tok")
    rows = block.shape[0]
    if count != 8:
        whole = lax.all_gather(block, "tok", axis=0, tiled=True)
        return [[(whole, i * rows, rows)] for i in range(count)]
    _, second, partner = cube_routes()
    across = lax.ppermute(neighbours[0], "tok", second)
    every = jnp.concatenate(after([block, *neighbours, across], tie), axis=0)
    return [
        [(side, i * rows, rows)]
        for side in (every, lax.ppermute(every, "tok", partner))
        for i in range(4)
    ]


def flatten(blocks):
    arrays, spec = [], []
    for pieces in blocks:
        here = []
        for array, first, rows in pieces:
            known = [i for i, other in enumerate(arrays) if other is array]
            if not known:
                known = [len(arrays)]
                arrays.append(array)
            here.append((known[0], first, rows))
        spec.append(here)
    return arrays, spec


def row_ranges(pieces, first, count):
    base = 0
    for array, start, rows in pieces:
        low, high = max(first, base), min(first + count, base + rows)
        if low < high:
            yield array, start + low - base, low - first, high - low
        base += rows


def after(value, tie):
    return value if tie is None else lax.optimization_barrier((value, tie))[0]


def plane_sum(near, far, last, rows):
    first, second, partner = cube_routes()
    half = rows // 2
    got_last = lax.ppermute(last, "tok", partner)
    got = lax.ppermute(far, "tok", partner)
    three = (near[3 * rows :].astype(F32) + got_last.astype(F32)).astype(BF16)
    across_upper = lax.ppermute(three[:half], "tok", second)
    across_lower = lax.ppermute(three[half:], "tok", first)
    near, got = after((near, got), (across_upper, across_lower))

    def pair(block):
        here = slice(block * rows, (block + 1) * rows)
        return near[here].astype(F32) + got[here].astype(F32)

    nothing = jnp.zeros(across_upper.shape, F32)
    add_upper = jnp.concatenate([across_upper.astype(F32), nothing], axis=0)
    add_lower = jnp.concatenate([nothing, across_lower.astype(F32)], axis=0)
    along = lax.ppermute((pair(1) + add_upper).astype(BF16), "tok", first)
    beside = lax.ppermute((pair(2) + add_lower).astype(BF16), "tok", second)
    return pair(0) + beside.astype(F32) + along.astype(F32)


BEGIN, PLACE, BLOCK = 120, 121, 122


def table_kernel(groups, me, owner_of, fill_of, group_ids, inverse, segs, *outs):
    cosines, sines, info, marks = outs[:2], outs[2:4], outs[4], outs[5]
    ids = group_ids[...]
    owner = jnp.zeros(ids.shape, F32)
    fill = jnp.zeros(ids.shape, F32)
    for g in range(owner_of.shape[0]):
        owner = jnp.where(ids == g, owner_of[g].astype(F32), owner)
        fill = jnp.where(ids == g, fill_of[owner_of[g]].astype(F32), fill)
    square = (LANES, LANES)
    row = lax.broadcasted_iota(jnp.int32, square, 0)
    lane = lax.broadcasted_iota(jnp.int32, square, 1)
    request = lax.broadcasted_iota(jnp.int32, (LANES, ids.shape[1]), 1).astype(F32)
    sign = jnp.where(lane % HS < HS // 2, -1.0, 1.0)
    many = segs.shape[0]
    for j in range(groups):
        block = lax.rem(me[1] - j + groups, groups)
        which = me[0] * groups + block
        here = segs[pl.ds(which, 1), :].astype(F32)
        own = jnp.sum(jnp.where(row == lane, here, 0.0), axis=1, keepdims=True)
        wide = jnp.broadcast_to(own, square)
        earlier = jnp.zeros(square, F32)
        for u in range(many):
            earlier += jnp.where(segs[u : u + 1, :].astype(F32) < wide, 1.0, 0.0)
        begin = jnp.sum(earlier, axis=1, keepdims=True)
        match = own == request
        slab = jnp.sum(jnp.where(match, owner, 0.0), axis=1, keepdims=True)
        start = jnp.sum(jnp.where(match, fill, 0.0), axis=1, keepdims=True)
        first = which * LANES
        place = (first + row).astype(F32)
        angles = (start + place - begin) * inverse[...]
        side, at = (0, j) if j < groups // 2 else (1, j - groups // 2)
        cosines[side][at * LANES : (at + 1) * LANES, :] = jnp.cos(angles)
        sines[side][at * LANES : (at + 1) * LANES, :] = jnp.sin(angles) * sign
        slab_wide = jnp.broadcast_to(slab, square).astype(jnp.int32)
        begin_wide = jnp.broadcast_to(begin, square)
        info[j, 0] = slab_wide
        info[j, 1] = begin_wide.astype(jnp.int32)
        read = jnp.max(jnp.where(slab_wide == lane, 1.0, 0.0), axis=0, keepdims=True)
        lowest = jnp.min(begin_wide, axis=0, keepdims=True)
        spot = lane[:1]
        line = jnp.where(spot == BEGIN, lowest, read).astype(jnp.int32)
        line = jnp.where(spot == PLACE, first, line)
        marks[j : j + 1, :] = jnp.where(spot == BLOCK, block, line)


def row_tables(groups, me, prefix_owner, slab_fill, group_ids, inverse, segments):
    half = jax.ShapeDtypeStruct((groups // 2 * LANES, LANES), F32)
    outs = pl.pallas_call(
        functools.partial(table_kernel, groups),
        out_shape=(half,) * 4
        + (
            jax.ShapeDtypeStruct((groups, 2, LANES, LANES), jnp.int32),
            jax.ShapeDtypeStruct((groups, LANES), jnp.int32),
        ),
        in_specs=[SMEM] * 3 + [vmem()] * 3,
        out_specs=(vmem(),) * 6,
        compiler_params=params(),
        cost_estimate=pl.CostEstimate(
            flops=4 * 10**9, bytes_accessed=10**6, transcendentals=10**5
        ),
        name="row_tables",
    )(
        me,
        prefix_owner,
        slab_fill,
        group_ids.reshape(1, -1),
        inverse.reshape(1, LANES),
        segments.reshape(-1, LANES),
    )
    return outs[:2], outs[2:4], outs[4], outs[5]


def project_kernel(blocks, kv_local, q_local, *refs):
    pieces = refs[: 2 * blocks]
    gain, wq, wkv, cos, sin = refs[2 * blocks : 2 * blocks + 5]
    q_outs = refs[2 * blocks + 5 : 3 * blocks + 5]
    kv_out, normed = refs[3 * blocks + 5 :]
    half = pieces[0].shape[0]
    for i, piece in enumerate(pieces):
        wide = piece[...].astype(F32)
        spread = jnp.mean(wide * wide, axis=-1, keepdims=True)
        normed[i * half : (i + 1) * half, :] = (
            wide * lax.rsqrt(spread + NORM_EPS) * gain[...]
        ).astype(BF16)
    share = q_local // kv_local
    rows = normed.shape[0]
    rows_dev = rows // blocks
    lane = lax.broadcasted_iota(jnp.int32, (rows, LANES), 1)
    low_half = lane % HS < HS // 2
    low_head = lane < HS

    def turned(values, cosine, sine):
        swapped = jnp.where(
            low_half, pltpu.roll(values, LANES - HS // 2, 1), pltpu.roll(values, HS // 2, 1)
        )
        return values * cosine + swapped * sine

    cosine = cos[...]
    sine = sin[...]
    keyval = jnp.dot(normed[...], wkv[...], preferred_element_type=F32)
    cosine_kv = jnp.where(low_head, cosine, 1.0)
    sine_kv = jnp.where(low_head, sine, 0.0)
    for g in range(kv_local):
        here = slice(g * LANES, (g + 1) * LANES)
        kv_out[:, here] = turned(keyval[:, here], cosine_kv, sine_kv).astype(BF16)
    queries = jnp.dot(normed[...], wq[...], preferred_element_type=F32)
    for pair in range(queries.shape[1] // LANES):
        both = turned(queries[:, pair * LANES : (pair + 1) * LANES], cosine, sine) * HS ** (-0.5)
        for odd in range(2):
            head = 2 * pair + odd
            if head >= q_local:
                continue
            alone = pltpu.roll(both, HS, 1) if odd else both
            alone = jnp.where(low_head, alone, 0.0).astype(BF16)
            group, slot = head // share, head % share
            for j in range(blocks):
                q_outs[j][group, slot * rows_dev : (slot + 1) * rows_dev, :] = alone[
                    j * rows_dev : (j + 1) * rows_dev
                ]


def project(pieces, gain, w_query, w_keyval, cos, sin, kv_local, q_local):
    blocks = len(pieces) // 2
    rows_dev, width = 2 * pieces[0].shape[0], pieces[0].shape[1]
    share = q_local // kv_local
    outs = pl.pallas_call(
        functools.partial(project_kernel, blocks, kv_local, q_local),
        out_shape=[jax.ShapeDtypeStruct((kv_local, share * rows_dev, LANES), BF16)] * blocks
        + [jax.ShapeDtypeStruct((blocks * rows_dev, kv_local * LANES), BF16)],
        in_specs=[vmem()] * (2 * blocks + 5),
        out_specs=[vmem()] * (blocks + 1),
        scratch_shapes=[pltpu.VMEM((blocks * rows_dev, width), BF16)],
        compiler_params=params(),
        cost_estimate=pl.CostEstimate(
            flops=4 * 10**9, bytes_accessed=4 * 10**6, transcendentals=blocks * rows_dev
        ),
        name="norm_project_rotate",
    )(*pieces, gain, w_query, w_keyval, cos, sin)
    return list(outs[:-1]), outs[-1]


def attend_kernel(block, near_parts, slab_spec, q_local, *refs):
    marks, slab_id, fill_of, query, info = refs[:5]
    near_refs = refs[5 : 5 + near_parts]
    slab_refs = refs[5 + near_parts : -18]
    w_ref, out = refs[-18:-16]
    near, far, scores, peak, total, accum, begin, owner, heads, mixed, w_all, held = refs[-16:-4]
    near_sems, slab_sems, w_sem, info_sem = refs[-4:]
    parts = info.shape[0]
    kv_local, stack, _ = query.shape
    rows_dev = info.shape[2]
    share = stack // rows_dev
    cuts = PREFIX // LANES
    window = parts + 1
    wide = (stack, LANES)
    lane = lax.broadcasted_iota(jnp.int32, (1, LANES), 1)

    def lanes(ref, g, rows, start=0):
        return ref.at[pl.ds(start, rows), pl.ds(g * LANES, LANES)]

    copies = []
    base = 0
    for i, ref in enumerate(near_refs):
        for g in range(kv_local):
            copies.append(
                pltpu.make_async_copy(
                    lanes(ref, g, ref.shape[0]),
                    near.at[g, pl.ds(base, ref.shape[0])],
                    near_sems.at[i, g],
                )
            )
        base += ref.shape[0]

    def each_slab(act):
        for i, [(array, start, _)] in enumerate(slab_spec):
            @pl.when(marks[block, slab_id[i]] != 0)
            def _(i=i, array=array, start=start):
                for g in range(kv_local):
                    act(
                        pltpu.make_async_copy(
                            lanes(slab_refs[array], g, PREFIX, start),
                            far.at[g, pl.ds(i * PREFIX, PREFIX)],
                            slab_sems.at[i, g],
                        )
                    )

    w_copy = pltpu.make_async_copy(w_ref, w_all, w_sem)
    info_copy = pltpu.make_async_copy(info.at[block], held, info_sem)
    info_copy.start()
    for copy in copies:
        copy.start()
    each_slab(lambda copy: copy.start())
    w_copy.start()
    info_copy.wait()
    for ref, kind in ((owner, 0), (begin, 1)):
        ref[...] = jnp.concatenate([held[kind]] * share, axis=0)
    row = lax.broadcasted_iota(jnp.int32, wide, 0)
    order = row - lax.div(row, rows_dev) * rows_dev
    for copy in copies:
        copy.wait()

    def rows_near(g, back):
        unit = lax.rem(block + back, parts) + jnp.where(marks[block, BLOCK] >= back, parts, 0)
        return near[g, pl.ds(pl.multiple_of(unit * rows_dev, rows_dev), rows_dev), :]

    def rows_window(g, backs):
        return jnp.concatenate([rows_near(g, back) for back in backs], axis=0)

    def rows_far(g, slab):
        return far[g, pl.ds(pl.multiple_of(slab * PREFIX, PREFIX), PREFIX), :]

    def score(g, rows):
        return lax.dot_general(
            query[g], rows, (((1,), (1,)), ((), ())), preferred_element_type=F32
        )

    def near_scores(backs, opening):
        for g in range(kv_local):
            every = score(g, rows_window(g, backs))
            top = None if opening else peak[g]
            for at, back in enumerate(backs):
                there = marks[block, PLACE] - back * rows_dev + lane
                seen = there >= begin[...]
                if back == 0:
                    seen = seen & (lane <= order)
                here = every[:, at * LANES : (at + 1) * LANES]
                here = jnp.where(seen, here, NEG_FILL)
                scores[g, back] = here
                top = here if top is None else jnp.maximum(top, here)
            peak[g] = top

    def far_scores(slab):
        mine = owner[...] == slab_id[slab]
        for g in range(kv_local):
            every = score(g, rows_far(g, slab))
            top = None
            for c in range(cuts):
                here = every[:, c * LANES : (c + 1) * LANES]
                if (c + 1) * LANES > PREFIX // 2:
                    here = jnp.where(lane + c * LANES < fill_of[slab_id[slab]], here, NEG_FILL)
                scores[g, window + slab * cuts + c] = here
                top = here if top is None else jnp.maximum(top, here)
            old = peak[g]
            peak[g] = jnp.where(mine, jnp.maximum(old, top), old)

    def near_values(backs, opening):
        for g in range(kv_local):
            weights = [jnp.exp(scores[g, back] - peak[g]) for back in backs]
            packed = jnp.concatenate([part.astype(BF16) for part in weights], axis=1)
            summed = functools.reduce(jnp.add, weights)
            product = jnp.dot(packed, rows_window(g, backs), preferred_element_type=F32)
            if opening:
                total[g] = summed
                accum[g] = product
            else:
                total[g] += summed
                accum[g] += product

    def far_values(slab):
        mine = owner[...] == slab_id[slab]
        for g in range(kv_local):
            shift = jnp.where(mine, peak[g], -NEG_FILL)
            weights = [
                jnp.exp(scores[g, window + slab * cuts + c] - shift) for c in range(cuts)
            ]
            packed = jnp.concatenate([part.astype(BF16) for part in weights], axis=1)
            total[g] += functools.reduce(jnp.add, weights)
            accum[g] += jnp.dot(packed, rows_far(g, slab), preferred_element_type=F32)

    def sweep(near_body, far_body, between=None):
        near_body((0, 1), True)

        @pl.when(marks[block, BEGIN] < marks[block, PLACE] - rows_dev)
        def _():
            near_body(tuple(range(2, window)), False)

        if between is not None:
            between()

        @pl.loop(0, len(slab_spec))
        def _(slab):
            @pl.when(marks[block, slab_id[slab]] != 0)
            def _():
                far_body(slab)

    sweep(near_scores, far_scores, lambda: each_slab(lambda copy: copy.wait()))
    for g in range(kv_local):
        peak[g] = jnp.broadcast_to(jnp.max(peak[g], axis=1, keepdims=True), wide)
    sweep(near_values, far_values)
    for g in range(kv_local):
        result = accum[g] / jnp.sum(total[g], axis=1, keepdims=True)
        for slot in range(share):
            heads[g * share + slot] = result[slot * rows_dev : (slot + 1) * rows_dev]

    low = lax.broadcasted_iota(jnp.int32, (rows_dev, LANES), 1) < HS
    for pair in range((q_local + 1) // 2):
        left = pltpu.roll(heads[2 * pair], HS, 1)
        here = slice(pair * LANES, (pair + 1) * LANES)
        if 2 * pair + 1 < q_local:
            mixed[:, here] = jnp.where(low, left, heads[2 * pair + 1]).astype(BF16)
        else:
            mixed[:, pair * LANES :] = left[:, :HS].astype(BF16)
    w_copy.wait()
    out[...] = jnp.dot(mixed[...], w_all[...], preferred_element_type=F32).astype(out.dtype)


def attend(block, marks, origins, slab_fill, info, query, near, slabs, w_out, q_local, held_as):
    parts = info.shape[0]
    kv_local, stack, _ = query.shape
    rows_dev = info.shape[2]
    units = parts + 1 + len(slabs) * (PREFIX // LANES)
    wide = (stack, LANES)
    arrays, slab_spec = flatten(slabs)
    return pl.pallas_call(
        functools.partial(attend_kernel, block, len(near), slab_spec, q_local),
        out_shape=jax.ShapeDtypeStruct((rows_dev, w_out.shape[1]), held_as),
        in_specs=[SMEM] * 3 + [vmem()] + [ANY] * (len(near) + len(arrays) + 2),
        out_specs=vmem(),
        scratch_shapes=[
            pltpu.VMEM((kv_local, 2 * parts * rows_dev, LANES), BF16),
            pltpu.VMEM((kv_local, len(slabs) * PREFIX, LANES), BF16),
            pltpu.VMEM((kv_local, units) + wide, F32),
            pltpu.VMEM((kv_local,) + wide, F32),
            pltpu.VMEM((kv_local,) + wide, F32),
            pltpu.VMEM((kv_local,) + wide, F32),
            pltpu.VMEM(wide, jnp.int32),
            pltpu.VMEM(wide, jnp.int32),
            pltpu.VMEM((q_local, rows_dev, LANES), F32),
            pltpu.VMEM((rows_dev, q_local * HS), BF16),
            pltpu.VMEM(w_out.shape, BF16),
            pltpu.VMEM(info.shape[1:], jnp.int32),
            pltpu.SemaphoreType.DMA((len(near), kv_local)),
            pltpu.SemaphoreType.DMA((len(slabs), kv_local)),
            pltpu.SemaphoreType.DMA,
            pltpu.SemaphoreType.DMA,
        ],
        compiler_params=params(),
        cost_estimate=pl.CostEstimate(
            flops=8 * 10**9, bytes_accessed=4 * 10**6, transcendentals=10**6
        ),
        name="attend",
    )(
        marks,
        origins,
        slab_fill,
        query,
        info,
        *near,
        *arrays,
        w_out,
    )


def hidden_kernel(tokens, gain, own, *refs):
    others = refs[:-2]
    hidden, expert_in = refs[-2:]
    total = tokens[...].astype(F32) + own[...]
    for other in others:
        total += other[...].astype(F32)
    hidden[...] = total
    spread = jnp.mean(total * total, axis=-1, keepdims=True)
    expert_in[...] = (total * lax.rsqrt(spread + NORM_EPS) * gain[...]).astype(BF16)


def add_and_norm(tokens, gain, own, others):
    return pl.pallas_call(
        hidden_kernel,
        out_shape=(
            jax.ShapeDtypeStruct(tokens.shape, F32),
            jax.ShapeDtypeStruct(tokens.shape, BF16),
        ),
        in_specs=[vmem()] * (3 + len(others)),
        out_specs=(vmem(), vmem()),
        compiler_params=params(),
        cost_estimate=pl.CostEstimate(
            flops=10**9, bytes_accessed=16 * tokens.size, transcendentals=tokens.shape[0]
        ),
        name="add_and_norm",
    )(tokens, gain, own, *others)


def expert_kernel(spec, rows, layout, slot_row, gate_row, slot_col, *refs):
    count = len(spec)
    x_refs = refs[: -12 - len(layout)]
    wg_ref, wu_ref, wd_ref = refs[-12 - len(layout) : -9 - len(layout)]
    outs = refs[-9 - len(layout) : -9]
    x_all, wg, wu, wd, picked, answered, inner, x_sem, w_sem = refs[-9:]
    targets = [(out, i) for out, many in zip(outs, layout) for i in range(many)]
    exp_local = wg.shape[0]
    width = x_all.shape[1]
    span = 2 * rows
    slots = 2 * CAP
    pairs = count // 2
    chunk = 512

    x_copies = []
    base = 0
    for array, there, many_rows in [piece for pieces in spec for piece in pieces]:
        x_copies.append(
            pltpu.make_async_copy(
                x_refs[array].at[pl.ds(there, many_rows)],
                x_all.at[pl.ds(base, many_rows)],
                x_sem.at[len(x_copies)],
            )
        )
        base += many_rows
    for copy in x_copies:
        copy.start()

    def w_copies(e):
        return [
            pltpu.make_async_copy(source.at[e], target.at[e], w_sem.at[e, i])
            for i, (source, target) in enumerate(((wg_ref, wg), (wu_ref, wu), (wd_ref, wd)))
        ]

    for e in range(exp_local):
        for copy in w_copies(e):
            copy.start()
    for copy in x_copies:
        copy.wait()

    slot_iota = lax.broadcasted_iota(jnp.int32, (slots, span), 0)

    def pair_hits(e, b):
        there = slice(b * span, (b + 1) * span)
        return slot_iota == slot_row[pl.ds(e, 1), there]

    for b in range(pairs):
        hits = [jnp.where(pair_hits(e, b), 1.0, 0.0).astype(BF16) for e in range(exp_local)]
        chooser = jnp.concatenate(hits, axis=0)
        for c in range(0, width, chunk):
            found = jnp.dot(
                chooser,
                x_all[b * span : (b + 1) * span, c : c + chunk],
                preferred_element_type=F32,
            ).astype(BF16)
            for e in range(exp_local):
                picked[e, b * slots : (b + 1) * slots, c : c + chunk] = found[
                    e * slots : (e + 1) * slots
                ]

    @pl.loop(0, exp_local)
    def _(e):
        for copy in w_copies(e):
            copy.wait()
        rows_in = picked[e]
        for c in range(0, inner.shape[1], 256):
            gate = jnp.dot(rows_in, wg[e, :, c : c + 256], preferred_element_type=F32)
            up = jnp.dot(rows_in, wu[e, :, c : c + 256], preferred_element_type=F32)
            inner[:, c : c + 256] = (gate / (1.0 + jnp.exp(-gate)) * up).astype(BF16)
        scale = jnp.concatenate(
            [
                jnp.sum(
                    jnp.where(
                        pair_hits(e, b),
                        gate_row[pl.ds(e, 1), b * span : (b + 1) * span],
                        0.0,
                    ),
                    axis=1,
                    keepdims=True,
                )
                for b in range(pairs)
            ],
            axis=0,
        )
        for c in range(0, width, chunk):
            answer = jnp.dot(inner[...], wd[e, :, c : c + chunk], preferred_element_type=F32)
            answer = (answer * scale).astype(BF16)
            for b in range(pairs):
                first = pl.multiple_of(e * slots, slots)
                answered[b, pl.ds(first, slots), c : c + chunk] = answer[
                    b * slots : (b + 1) * slots
                ]

    lane = lax.broadcasted_iota(jnp.int32, (span, slots), 1)
    for b in range(pairs):
        there = slice(b * span, (b + 1) * span)
        spreader = jnp.concatenate(
            [
                jnp.where(lane == slot_col[there, e : e + 1], 1.0, 0.0).astype(BF16)
                for e in range(exp_local)
            ],
            axis=1,
        )
        for c in range(0, width, chunk):
            sums = jnp.dot(
                spreader, answered[b, :, c : c + chunk], preferred_element_type=F32
            ).astype(BF16)
            for side in range(2):
                out, at = targets[2 * b + side]
                out[at * rows : (at + 1) * rows, c : c + chunk] = sums[
                    side * rows : (side + 1) * rows
                ]


def experts(blocks, layout, route, w_gate, w_up, w_down):
    count = len(blocks)
    pieces, spec = flatten(blocks)
    parts = sum(len(one) for one in spec)
    rows, width = blocks[0][0][2], pieces[0].shape[1]
    exp_local, _, hidden = w_gate.shape
    pairs = count // 2
    slots = 2 * CAP
    work = exp_local * pairs * slots
    return pl.pallas_call(
        functools.partial(expert_kernel, spec, rows, layout),
        out_shape=tuple(
            jax.ShapeDtypeStruct((many * rows, width), BF16)
            for many in layout
        ),
        in_specs=[vmem()] * 3 + [ANY] * (len(pieces) + 3),
        out_specs=(vmem(),) * len(layout),
        scratch_shapes=[
            pltpu.VMEM((count * rows, width), BF16),
            pltpu.VMEM(w_gate.shape, BF16),
            pltpu.VMEM(w_up.shape, BF16),
            pltpu.VMEM(w_down.shape, BF16),
            pltpu.VMEM((exp_local, pairs * slots, width), BF16),
            pltpu.VMEM((pairs, exp_local * slots, width), BF16),
            pltpu.VMEM((pairs * slots, hidden), BF16),
            pltpu.SemaphoreType.DMA((parts,)),
            pltpu.SemaphoreType.DMA((exp_local, 3)),
        ],
        compiler_params=params(),
        cost_estimate=pl.CostEstimate(
            flops=2 * work * width * (3 * hidden + 4 * rows),
            bytes_accessed=2 * (3 * w_gate.size + 2 * count * rows * width),
            transcendentals=work * hidden,
        ),
        name="experts",
    )(*route, *pieces, w_gate, w_up, w_down)


def packed_routes(routes, route_gates, lanes):
    parts = [routes.T.astype(BF16)]
    rest = route_gates.T
    for _ in range(3):
        term = lax.reduce_precision(rest, 8, 7)
        parts.append(term.astype(BF16))
        rest = rest - term
    per = len(parts) * LANES // lanes
    return jnp.concatenate(
        [jnp.concatenate(parts[i : i + per], axis=0) for i in range(0, len(parts), per)], axis=1
    )


def route_kernel(spec, first_expert, *refs):
    count = len(spec)
    sources = refs[:-5]
    slot_row, gate_row, slot_col, packed, sems = refs[-5:]
    exp_local = slot_row.shape[0]
    tall = packed.shape[1]
    copies = [
        pltpu.make_async_copy(
            sources[array].at[pl.ds(there + rows - tall, tall), pl.ds(0, packed.shape[2])],
            packed.at[k],
            sems.at[k],
        )
        for k, (array, there, rows) in enumerate(pieces[-1] for pieces in spec)
    ]
    for copy in copies:
        copy.start()
    for copy in copies:
        copy.wait()
    here = lax.broadcasted_iota(jnp.int32, (LANES, LANES), 1)
    there = lax.broadcasted_iota(jnp.int32, (LANES, LANES), 0)
    earlier = jnp.where(there < here, 1.0, 0.0).astype(BF16)
    choices = tall * packed.shape[2] // (4 * LANES)
    for k in range(count):
        block = packed[k].astype(F32)
        parts = [
            block[r : r + choices, c : c + LANES]
            for c in range(0, packed.shape[2], LANES)
            for r in range(0, tall, choices)
        ]
        named = parts[0]
        gates = parts[1] + parts[2] + parts[3]
        hits, shares = [], []
        for e in range(exp_local):
            match = named == (first_expert[0] + e).astype(F32)
            hits.append(jnp.max(jnp.where(match, 1.0, 0.0), axis=0, keepdims=True))
            shares.append(jnp.sum(jnp.where(match, gates, 0.0), axis=0, keepdims=True))
        hits += [jnp.zeros((1, LANES), F32)] * (8 - exp_local)
        hit = jnp.concatenate(hits, axis=0)
        rank = jnp.dot(hit.astype(BF16), earlier, preferred_element_type=F32)
        slot = jnp.where(hit > 0.0, rank + float(k % 2 * CAP), -1.0)
        lanes = slice(k * LANES, (k + 1) * LANES)
        slot_row[:, lanes] = slot[:exp_local].astype(jnp.int32)
        gate_row[:, lanes] = jnp.concatenate(shares, axis=0)
        slot_col[lanes, :] = slot.T.astype(jnp.int32)


def route_tables(sources, tall, lanes, first_expert, exp_local):
    count = len(sources)
    sources, spec = flatten(sources)
    tokens = count * LANES
    return pl.pallas_call(
        functools.partial(route_kernel, spec),
        out_shape=(
            jax.ShapeDtypeStruct((exp_local, tokens), jnp.int32),
            jax.ShapeDtypeStruct((exp_local, tokens), F32),
            jax.ShapeDtypeStruct((tokens, 8), jnp.int32),
        ),
        in_specs=[SMEM] + [ANY] * len(sources),
        out_specs=(vmem(), vmem(), vmem()),
        scratch_shapes=[
            pltpu.VMEM((count, tall, lanes), BF16),
            pltpu.SemaphoreType.DMA((count,)),
        ],
        compiler_params=params(),
        cost_estimate=pl.CostEstimate(
            flops=3 * 10**9, bytes_accessed=10**6, transcendentals=0
        ),
        name="route_tables",
    )(first_expert, *sources)


def local(
    tokens,
    segments,
    group_ids,
    prefix_owner,
    slab_fill,
    prefix_cache,
    attn_gain,
    w_query,
    w_keyval,
    w_out,
    ffn_gain,
    routes,
    route_gates,
    w_gate,
    w_up,
    w_down,
):
    tok_count = lax.axis_size("tok")
    groups = lax.axis_size("head")
    me_tok = lax.axis_index("tok")
    me_head = lax.axis_index("head")
    rows_dev, width = tokens.shape
    kv_local = w_keyval.shape[1] // (2 * HS)
    q_local = w_query.shape[1] // HS
    origins = plane_origins()

    half = rows_dev // 2
    turns = [(tokens[:half], tokens[half:])]

    def turn_on(tie):
        turns.append(tuple(next_turn(after(part, tie), "head") for part in turns[-1]))

    for _ in range(groups // 2):
        turn_on(None)

    steps_idx = jnp.arange(HS // 2, dtype=F32)
    inverse = jnp.exp(steps_idx * (-2.0 * jnp.log(10000.0) / HS))
    cos, sin, info, marks = row_tables(
        groups,
        jnp.stack([me_tok, me_head]).astype(jnp.int32),
        prefix_owner,
        slab_fill,
        group_ids,
        jnp.concatenate([inverse] * 4),
        segments,
    )

    missing = -w_query.shape[1] % LANES
    if missing:
        w_query = jnp.pad(w_query, ((0, 0), (0, missing)))

    lanes = prefix_cache.shape[1]
    packed = packed_routes(routes, route_gates, lanes)
    prefix_rows = after(jnp.concatenate([prefix_cache, packed], axis=0), turns[1][0])
    neighbours = to_neighbours(prefix_rows)

    queries, own, prev = [], [], []
    for some in (slice(0, groups // 2), slice(groups // 2, groups)):
        while len(turns) < some.stop:
            turn_on((own[0], neighbours))
        pieces = [piece for parts in turns[some] for piece in parts]
        query, keyval = project(
            after(pieces, prev[0]) if prev else pieces,
            attn_gain[None, :],
            w_query,
            w_keyval,
            cos[len(own)],
            sin[len(own)],
            kv_local,
            q_local,
        )
        queries += query
        own.append(keyval)
        prev.append(lax.ppermute(keyval, "tok", [(i, i + 1) for i in range(tok_count - 1)]))

    def exchanged(block, j):
        return lax.ppermute(block, "head", [(i, (i - j) % groups) for i in range(groups)])

    cached = to_plane(prefix_rows, neighbours, own[1])

    near = prev + own

    def term(j, held_as):
        return attend(
            j, marks, origins, slab_fill, info, queries[j], near, cached, w_out, q_local, held_as
        )

    down = groups // 2
    up = groups - 1 - down
    lower = upper = None
    for turn in range(down):
        here = term(down - turn, BF16)
        if lower is not None:
            here = (here.astype(F32) + lower.astype(F32)).astype(BF16)
        lower = exchanged(here, 1)
        if turn < up:
            here = term(groups - up + turn, BF16)
            if upper is not None:
                here = (here.astype(F32) + upper.astype(F32)).astype(BF16)
            upper = exchanged(here, groups - 1)
    terms = [lower] if upper is None else [lower, upper]
    own_term = term(0, F32)
    exp_local = w_gate.shape[0]
    route = route_tables(
        cached,
        packed.shape[0],
        lanes,
        (me_tok * exp_local).astype(jnp.int32).reshape(1),
        exp_local,
    )
    hidden, expert_in = add_and_norm(tokens, ffn_gain[None, :], own_term, after(terms, route))

    def chosen(blocks, layout):
        return experts(blocks, layout, route, w_gate, w_up, w_down)

    if tok_count != 8:
        every = lax.all_gather(expert_in, "tok", axis=0, tiled=True)
        blocks = [[(every, k * rows_dev, rows_dev)] for k in range(tok_count)]
        (sums,) = chosen(blocks, (tok_count,))
        summed = lax.psum_scatter(sums, "tok", scatter_dimension=0, tiled=True).astype(F32)
        return (hidden + summed).astype(BF16)

    first, second, partner = cube_routes()

    def to_partner(array):
        return lax.ppermute(array, "tok", partner)

    one = lax.ppermute(expert_in, "tok", first)
    two = lax.ppermute(expert_in, "tok", second)
    three = [
        lax.ppermute(one[:half], "tok", second),
        lax.ppermute(two[half:], "tok", first),
    ]
    mine = [[expert_in], [one], [two], three]
    blocks = [
        [(piece, 0, piece.shape[0]) for piece in pieces]
        for pieces in mine + [[to_partner(piece) for piece in pieces] for pieces in mine]
    ]
    near, far, last = chosen(blocks, (4, 3, 1))
    return (hidden + plane_sum(near, far, last, rows_dev)).astype(BF16)


def solution(mesh):
    return jax.shard_map(
        local,
        mesh=mesh,
        in_specs=(
            P(("tok", "head"), None),
            P(),
            P(),
            P(),
            P(),
            P("tok", "head"),
            P(),
            P(None, "head"),
            P(None, "head"),
            P("head", None),
            P(),
            P(("tok", "head"), None),
            P(("tok", "head"), None),
            P("tok", None, None),
            P("tok", None, None),
            P("tok", None, None),
        ),
        out_specs=P(("tok", "head"), None),
        check_vma=False,
    )
```
